32 devices in a mesh: cand: 2 (over y), gx: 4 (over z), gy: 2 (over x), gz: 2 (over core).
Axes of the slice: x: 2, y: 2, z: 4, core: 2. Of those that a mesh axis runs over, the one named last changes fastest.
Arguments:
- tokens: bfloat16 [64, 64, 16, 128], P(('cand', 'gx'), 'gy', 'gz'), parts along dimension 0, may hold values from -6 to 6
- region: int32 [64, 64, 16], P(('cand', 'gx'), 'gy', 'gz'), parts along dimension 0, may hold values from 0 to 2
- rel_index: int32 [256, 256], replicated, may hold values from 0 to 1574
- bias_table: float32 [1575, 4], replicated, may hold values from -3 to 303
- gain_attn: float32 [128], replicated, may hold values from 0.25 to 1.75
- w_qkv: bfloat16 [128, 384], replicated, may hold values from -0.5 to 0.5
- w_proj: bfloat16 [128, 128], replicated, may hold values from -0.5 to 0.5
- gain_mlp: float32 [128], replicated, may hold values from 0.25 to 1.75
- w_up: bfloat16 [128, 512], replicated, may hold values from -0.5 to 0.5
- w_down: bfloat16 [512, 128], replicated, may hold values from -0.25 to 0.25
Outputs:
- result: bfloat16 [64, 64, 16, 128], P(('cand', 'gx'), 'gy', 'gz'), parts along dimension 0
The draws below stay inside these ranges and needn't reach their ends.
There are 2 independent parts, one for each index of `cand`. The reference program is written for one: setup_inputs(seed, part) draws one part's arguments, and reference() takes and returns one part's arrays. A program takes and returns all parts, laid end to end along the dimension named above; an argument that names none is the same for every part. Nothing has to cross between parts.
All inputs are finite; a program needn't handle non-finite values.
Results may differ from the reference program's by a relative error of at most 0.0065.
Values may be sent and summed in bfloat16 or wider, within the bound.
No kernel may reach another device: no remote copies, remote signals or barrier semaphores. Data moves between devices by JAX's collectives and lax.ppermute only.
A program may use at most 128 MiB of HBM per device.

```python
import math
import jax
import jax.numpy as jnp
from jax import lax

D = 128
HEADS = 4
MLP = 512
WX = 8
WY = 8
WZ = 4
SX = 4
SY = 4
SZ = 2
WTOK = 256
RELS = 1575
NX = 32
NY = 64
NZ = 16


def draw_bias_table(key, part):
    key = jax.random.fold_in(key, 7)
    first = jax.random.fold_in(key, 0)
    return jnp.clip(jax.random.normal(first, (RELS, HEADS), jnp.float32), -3.0, 3.0)


def set_ends(array, stream_key, smallest, high):
    place = [jax.random.randint(jax.random.fold_in(stream_key, axis), (), 0, length) for axis, length in enumerate(array.shape)]
    widest = array.shape.index(max(array.shape))
    beside = place[:widest] + [(place[widest] + 1) % array.shape[widest]] + place[widest + 1:]
    return array.at[tuple(place)].set(smallest).at[tuple(beside)].set(high)


def block_scale(rng, extent, shards, low, high):
    loudness, own = 1.0, jax.random.fold_in(rng, 6)
    for axis_at, parts in shards:
        draws = jnp.exp(jax.random.uniform(jax.random.fold_in(own, axis_at), (parts,), jnp.float32, low / len(shards), high / len(shards)))
        loudness = loudness * jnp.repeat(draws, extent[axis_at] // parts).reshape([-1 if axis == axis_at else 1 for axis in range(len(extent))])
    return loudness


def normal_values(rng, dims, scale, reach, cuts=(), held_as=jnp.bfloat16):
    result = scale * jax.random.normal(rng, dims, jnp.float32)
    if cuts:
        result = result * block_scale(rng, dims, cuts, -0.22, 0.18)
    return jnp.clip(result, -reach, reach).astype(held_as)


def setup_inputs(seed: int = 0, part: int = 0) -> dict:
    arg_keys = jax.random.split(jax.random.key(seed), 11)
    own_keys = jax.random.split(jax.random.fold_in(arg_keys[10], part), 11)
    tokens = normal_values(own_keys[0], (NX, NY, NZ, D), 1.0, 6.0, ((0, 4), (1, 2), (2, 2)))
    region = set_ends(jax.random.randint(own_keys[1], (NX, NY, NZ), 0, 3), jax.random.fold_in(own_keys[1], 1), 0, 2).astype(jnp.int32)
    rel_index = set_ends(jax.random.randint(arg_keys[2], (WTOK, WTOK), 0, RELS), jax.random.fold_in(arg_keys[2], 1), 0, RELS - 1).astype(jnp.int32)
    bias_table = draw_bias_table(jax.random.fold_in(arg_keys[10], 71), part)
    gain_attn = jnp.clip(1.0 + 0.15 * jax.random.normal(arg_keys[4], (D,), jnp.float32), 0.25, 1.75)
    w_qkv = normal_values(arg_keys[5], (D, 3 * D), D ** -0.5, 0.5)
    w_proj = normal_values(arg_keys[6], (D, D), D ** -0.5, 0.5)
    gain_mlp = jnp.clip(1.0 + 0.15 * jax.random.normal(arg_keys[7], (D,), jnp.float32), 0.25, 1.75)
    w_up = normal_values(arg_keys[8], (D, MLP), D ** -0.5, 0.5)
    w_down = normal_values(arg_keys[9], (MLP, D), MLP ** -0.5, 0.25)
    return {"tokens": tokens, "region": region, "rel_index": rel_index, "bias_table": bias_table, "gain_attn": gain_attn, "w_qkv": w_qkv, "w_proj": w_proj, "gain_mlp": gain_mlp, "w_up": w_up, "w_down": w_down}


def layer_norm(values, norm_gain):
    center = values - lax.optimization_barrier(jnp.mean(values, axis=-1, keepdims=True))
    spread = lax.optimization_barrier(jnp.mean(center * center, axis=-1, keepdims=True))
    return center * lax.rsqrt(spread + 1e-05) * norm_gain.astype(jnp.float32)

def to_windows(volume):
    size_x, size_y, size_z, width = volume.shape
    parted = volume.reshape(size_x // WX, WX, size_y // WY, WY, size_z // WZ, WZ, width)
    return parted.transpose(0, 2, 4, 1, 3, 5, 6).reshape(-1, WX * WY * WZ, width)

def from_windows(windows, size_x, size_y, size_z):
    width = windows.shape[-1]
    parted = windows.reshape(size_x // WX, size_y // WY, size_z // WZ, WX, WY, WZ, width)
    return parted.transpose(0, 3, 1, 4, 2, 5, 6).reshape(size_x, size_y, size_z, width)

def attend(windows, labels, gain_attn, w_qkv, w_proj, bias_all):
    batch, length, width = windows.shape
    head_size = width // HEADS
    normed = layer_norm(windows.astype(jnp.float32), gain_attn).astype(jnp.bfloat16)
    qkv = jnp.dot(normed.reshape(batch * length, width), w_qkv, preferred_element_type=jnp.float32)
    qkv = qkv.astype(jnp.bfloat16).reshape(batch, length, 3, HEADS, head_size)
    query = qkv[:, :, 0].astype(jnp.float32)
    keys = qkv[:, :, 1].astype(jnp.float32)
    values = qkv[:, :, 2].astype(jnp.float32)
    scores = jnp.einsum('bihe,bjhe->bhij', query, keys) * head_size ** (-0.5) + bias_all[None]
    same = labels[:, :, None] == labels[:, None, :]
    scores = jnp.where(same[:, None], scores, -1000000000.0)
    peak_score = lax.optimization_barrier(jnp.max(scores, axis=-1, keepdims=True))
    weights = jnp.exp(scores - peak_score)
    probs = (weights / lax.optimization_barrier(jnp.sum(weights, axis=-1, keepdims=True))).astype(jnp.bfloat16)
    attended = jnp.einsum('bhij,bjhe->bihe', probs.astype(jnp.float32), values)
    attended = attended.astype(jnp.bfloat16).reshape(batch * length, width)
    projected = jnp.dot(attended, w_proj, preferred_element_type=jnp.float32)
    flat = windows.reshape(batch * length, width).astype(jnp.float32)
    return (flat + projected).astype(jnp.bfloat16)

def feed_forward(middle, gain_mlp, w_up, w_down):
    normed = layer_norm(middle.astype(jnp.float32), gain_mlp).astype(jnp.bfloat16)
    hidden = jax.nn.gelu(jnp.dot(normed, w_up, preferred_element_type=jnp.float32), approximate=False)
    hidden = hidden.astype(jnp.bfloat16)
    return (middle.astype(jnp.float32) + jnp.dot(hidden, w_down, preferred_element_type=jnp.float32)).astype(jnp.bfloat16)

def reference(tokens, region, rel_index, bias_table, gain_attn, w_qkv, w_proj, gain_mlp, w_up, w_down):
    size_x, size_y, size_z, width = tokens.shape
    shifted = jnp.roll(tokens, (-SX, -SY, -SZ), axis=(0, 1, 2))
    windows = to_windows(shifted)
    labels = to_windows(region[..., None])[..., 0]
    bias_all = jnp.transpose(bias_table[rel_index], (2, 0, 1)).astype(jnp.float32)
    number = windows.shape[0]
    length = windows.shape[1]
    bundle = math.gcd(number, 16)
    grouped = windows.reshape(number // bundle, bundle, length, width)
    grouped_labels = labels.reshape(number // bundle, bundle, length)

    def one_bundle(pieces):
        middle = attend(pieces[0], pieces[1], gain_attn, w_qkv, w_proj, bias_all)
        after = feed_forward(middle, gain_mlp, w_up, w_down)
        return after.reshape(bundle, length, width)
    outcome = lax.map(one_bundle, (grouped, grouped_labels)).reshape(number, length, width)
    after_field = from_windows(outcome, size_x, size_y, size_z)
    return jnp.roll(after_field, (SX, SY, SZ), axis=(0, 1, 2))
```

```python
import functools

import jax
import jax.numpy as jnp
from jax import lax
from jax.experimental import pallas as pl
from jax.experimental.pallas import tpu as pltpu
from jax.sharding import PartitionSpec as P

HEADS = 4
WX = 8
WY = 8
WZ = 4
SX = 4
SY = 4
SZ = 2
WTOK = WX * WY * WZ
LANES = 128
F32 = jnp.float32
BF16 = jnp.bfloat16
LOG2E = 1.4426950408889634


def shifted_2(value, axis, steps):
    count = lax.axis_size(axis)
    pairs = [(source, (source + steps) % count) for source in range(count)]
    return lax.ppermute(value, axis, pairs)


def to_windows(volume):
    size_x, size_y, size_z, width = volume.shape
    parted = volume.reshape(size_x // WX, WX, size_y // WY, WY, size_z // WZ, WZ, width)
    return parted.transpose(0, 2, 4, 1, 3, 5, 6).reshape(-1, WX * WY * WZ, width)


def from_windows(windows, size_x, size_y, size_z):
    width = windows.shape[-1]
    parted = windows.reshape(size_x // WX, size_y // WY, size_z // WZ, WX, WY, WZ, width)
    return parted.transpose(0, 3, 1, 4, 2, 5, 6).reshape(size_x, size_y, size_z, width)


def roll_along(volume, axis, name, steps, sign):
    size = volume.shape[axis]
    if sign < 0:
        piece = lax.slice_in_dim(volume, 0, steps, axis=axis)
        rest = lax.slice_in_dim(volume, steps, size, axis=axis)
        return jnp.concatenate([rest, shifted_2(piece, name, -1)], axis=axis)
    piece = lax.slice_in_dim(volume, size - steps, size, axis=axis)
    rest = lax.slice_in_dim(volume, 0, size - steps, axis=axis)
    return jnp.concatenate([shifted_2(piece, name, 1), rest], axis=axis)


def bias_kernel(index_ref, table_ref, bias_ref):
    chunks = table_ref.shape[1]
    index = index_ref[...].astype(F32).T.astype(jnp.int32)
    for column in range(0, WTOK, LANES):
        for row in range(0, WTOK, 8):
            part = index[row : row + 8, column : column + LANES]
            low = part & (LANES - 1)
            high = part >> 7
            found = [jnp.zeros((8, LANES), F32) for _ in range(HEADS)]
            for chunk in range(chunks):
                here = high == chunk
                for head in range(HEADS):
                    line = jnp.broadcast_to(table_ref[head, chunk : chunk + 1, :], (8, LANES))
                    got = jnp.take_along_axis(line, low, axis=1, mode="promise_in_bounds")
                    found[head] = jnp.where(here, got, found[head])
            for head in range(HEADS):
                bias_ref[head, row : row + 8, column : column + LANES] = found[head] * LOG2E


def gather_bias(rel_index, bias_table):
    rows = bias_table.shape[0]
    chunks = -(-rows // LANES)
    table = jnp.pad(bias_table.T, ((0, 0), (0, chunks * LANES - rows))).reshape(HEADS, chunks, LANES)
    return pl.pallas_call(
        bias_kernel,
        out_shape=jax.ShapeDtypeStruct((HEADS, WTOK, WTOK), F32),
        compiler_params=pltpu.CompilerParams(vmem_limit_bytes=32 << 20),
        name="gather_bias",
    )(rel_index, table)


def dot_nn(left, right):
    return lax.dot_general(left, right, (((1,), (0,)), ((), ())), preferred_element_type=F32)


def dot_nt(left, right):
    return lax.dot_general(left, right, (((1,), (1,)), ((), ())), preferred_element_type=F32)


def eye(size):
    rows = lax.broadcasted_iota(jnp.int32, (size, size), 0)
    columns = lax.broadcasted_iota(jnp.int32, (size, size), 1)
    return (rows == columns).astype(BF16)


def gelu(value):
    return 0.5 * value * (1.0 + lax.erf(value * (0.5**0.5)))


def block_kernel(
    x_ref, label_ref, bias_ref, gain_attn_ref, w_qkv_ref, w_v_t_ref, w_q_t_ref, w_proj_t_ref,
    gain_mlp_ref, w_up_t_ref, w_down_t_ref, out_ref,
):
    count = x_ref.shape[0]
    width = x_ref.shape[2]
    size = width // HEADS
    scale = size**-0.5 * LOG2E
    eye_width = eye(width)
    eye_window = eye(WTOK)
    for at in range(count):
        x16 = x_ref[at]
        x = x16.astype(F32)
        center = x - jnp.mean(x, axis=1, keepdims=True)
        spread = jnp.mean(center * center, axis=1, keepdims=True)
        normed = (center * lax.rsqrt(spread + 1e-05) * gain_attn_ref[...]).astype(BF16)
        x_t = dot_nt(eye_width, x16)
        q_t = dot_nt(w_q_t_ref[...], normed).astype(BF16)
        v_t = dot_nt(w_v_t_ref[...], normed).astype(BF16)
        k = dot_nn(normed, w_qkv_ref[:, width : 2 * width]).astype(BF16)
        row = label_ref[at]
        column = dot_nt(eye_window, jnp.broadcast_to(row.astype(BF16), (WTOK, WTOK)))
        same = column == row
        parts = []
        for head in range(HEADS):
            span = slice(head * size, (head + 1) * size)
            scores = dot_nn(k[:, span], q_t[span]) * scale + bias_ref[head]
            scores = jnp.where(same, scores, -1e9 * LOG2E)
            weights = jnp.exp2(scores - jnp.max(scores, axis=0, keepdims=True))
            total = jnp.sum(weights, axis=0, keepdims=True)
            part = dot_nn(v_t[span], weights.astype(BF16))
            parts.append((part * (1.0 / total)).astype(BF16))
        attended = jnp.concatenate(parts, axis=0)
        middle = (x_t + dot_nn(w_proj_t_ref[...], attended)).astype(BF16).astype(F32)
        center = middle - jnp.mean(middle, axis=0, keepdims=True)
        spread = jnp.mean(center * center, axis=0, keepdims=True)
        normed = (center * lax.rsqrt(spread + 1e-05) * gain_mlp_ref[...]).astype(BF16)
        hidden = gelu(dot_nn(w_up_t_ref[...], normed)).astype(BF16)
        after = (middle + dot_nn(w_down_t_ref[...], hidden)).astype(BF16)
        out_ref[at] = dot_nt(eye_window, after).astype(BF16)


def window_block(windows, labels, bias, gain_attn, w_qkv, w_proj, gain_mlp, w_up, w_down):
    number, length, width = windows.shape
    step = 2
    whole = lambda a: pl.BlockSpec(a.shape, lambda i: (0,) * a.ndim)
    fixed = (
        bias,
        gain_attn[None],
        w_qkv,
        w_qkv[:, 2 * width :].T,
        w_qkv[:, :width].T,
        w_proj.T,
        gain_mlp[:, None],
        w_up.T,
        w_down.T,
    )
    return pl.pallas_call(
        block_kernel,
        grid=(number // step,),
        in_specs=[
            pl.BlockSpec((step, length, width), lambda i: (i, 0, 0)),
            pl.BlockSpec((step, 1, length), lambda i: (i, 0, 0)),
        ]
        + [whole(a) for a in fixed],
        out_specs=pl.BlockSpec((step, length, width), lambda i: (i, 0, 0)),
        out_shape=jax.ShapeDtypeStruct((number, length, width), BF16),
        compiler_params=pltpu.CompilerParams(vmem_limit_bytes=48 << 20),
        name="window_block",
    )(windows, labels, *fixed)


def per_device(
    tokens, region, rel_index, bias_table, gain_attn, w_qkv, w_proj, gain_mlp, w_up, w_down
):
    size_x, size_y, size_z, width = tokens.shape
    shifted = roll_along(tokens, 0, "gx", SX, -1)
    shifted = roll_along(shifted, 1, "gy", SY, -1)
    shifted = roll_along(shifted, 2, "gz", SZ, -1)
    bias = gather_bias(rel_index, bias_table)
    windows = to_windows(shifted)
    labels = to_windows(region[..., None])[..., 0].astype(F32)[:, None, :]
    after = window_block(
        windows, labels, bias, gain_attn, w_qkv, w_proj, gain_mlp, w_up, w_down
    )
    field = from_windows(after, size_x, size_y, size_z)
    field = roll_along(field, 2, "gz", SZ, 1)
    field = roll_along(field, 1, "gy", SY, 1)
    return roll_along(field, 0, "gx", SX, 1)


def solution(mesh):
    field = P(("cand", "gx"), "gy", "gz", None)
    placed = (field, P(("cand", "gx"), "gy", "gz")) + (P(),) * 8
    return jax.shard_map(
        per_device, mesh=mesh, in_specs=placed, out_specs=field, check_vma=False
    )
```

```python
import math

import jax
import jax.numpy as jnp
from jax import lax
from jax.experimental import pallas as pl
from jax.experimental.pallas import tpu as pltpu
from jax.sharding import PartitionSpec as P

HEADS = 4
WX = 8
WY = 8
WZ = 4
SX = 4
SY = 4
SZ = 2
WTOK = WX * WY * WZ
LANES = 128
F32 = jnp.float32
BF16 = jnp.bfloat16
LOG2E = 1.4426950408889634


def prepare_kernel(
    index_ref, table_ref, w_qkv_ref, w_proj_ref, w_up_ref, w_down_ref,
    bias_ref, w_qv_t_ref, w_k_ref, w_proj_t_ref, w_up_t_ref, w_down_t_ref,
):
    width = w_proj_ref.shape[0]
    w_qv_t_ref[:width] = w_qkv_ref[:, :width].T
    w_qv_t_ref[width:] = w_qkv_ref[:, 2 * width :].T
    w_k_ref[...] = w_qkv_ref[:, width : 2 * width]
    w_proj_t_ref[...] = w_proj_ref[...].T
    w_up_t_ref[...] = w_up_ref[...].T
    w_down_t_ref[...] = w_down_ref[...].T
    chunks = table_ref.shape[1]
    index = index_ref[...].astype(F32).T.astype(jnp.int32)
    for column in range(0, WTOK, LANES):
        for row in range(0, WTOK, 8):
            part = index[row : row + 8, column : column + LANES]
            low = part & (LANES - 1)
            high = part >> 7
            found = [jnp.zeros((8, LANES), F32) for _ in range(HEADS)]
            for chunk in range(chunks):
                here = high == chunk
                for head in range(HEADS):
                    line = jnp.broadcast_to(table_ref[head, chunk : chunk + 1, :], (8, LANES))
                    got = jnp.take_along_axis(line, low, axis=1, mode="promise_in_bounds")
                    found[head] = jnp.where(here, got, found[head])
            for head in range(HEADS):
                bias_ref[head, row : row + 8, column : column + LANES] = found[head] * LOG2E


def prepare(rel_index, bias_table, w_qkv, w_proj, w_up, w_down):
    rows = bias_table.shape[0]
    width, hidden = w_up.shape
    chunks = -(-rows // LANES)
    table = jnp.pad(bias_table.T, ((0, 0), (0, chunks * LANES - rows))).reshape(HEADS, chunks, LANES)
    shapes = [(2 * width, width), (width, width), (width, width), (hidden, width), (width, hidden)]
    return pl.pallas_call(
        prepare_kernel,
        out_shape=[jax.ShapeDtypeStruct((HEADS, WTOK, WTOK), F32)]
        + [jax.ShapeDtypeStruct(shape, BF16) for shape in shapes],
        cost_estimate=cost(4),
        compiler_params=pltpu.CompilerParams(vmem_limit_bytes=32 << 20),
        name="bias_and_weights",
    )(rel_index, table, w_qkv, w_proj, w_up, w_down)


def dot_nn(left, right):
    return lax.dot_general(left, right, (((1,), (0,)), ((), ())), preferred_element_type=F32)


def dot_nt(left, right):
    return lax.dot_general(left, right, (((1,), (1,)), ((), ())), preferred_element_type=F32)


def eye(size):
    rows = lax.broadcasted_iota(jnp.int32, (size, size), 0)
    columns = lax.broadcasted_iota(jnp.int32, (size, size), 1)
    return (rows == columns).astype(BF16)


def gelu(value):
    return 0.5 * value * (1.0 + lax.erf(value * (0.5**0.5)))


HALF = SX * WY * WZ
EDGE = HALF // 2


def moved(value, axis, steps):
    names = (axis,) if isinstance(axis, str) else tuple(axis)
    moves = (steps,) if isinstance(axis, str) else tuple(steps)
    counts = [lax.axis_size(name) for name in names]
    pairs = []
    for source in range(math.prod(counts)):
        left, target, stride = source, 0, 1
        for count, move in zip(reversed(counts), reversed(moves)):
            target += (left % count + move) % count * stride
            left //= count
            stride *= count
        pairs.append((source, target))
    return lax.ppermute(value, names, pairs)


def turned(value, steps):
    return pltpu.roll(value, steps % 8, axis=1)


def sublane(shape):
    return lax.broadcasted_iota(jnp.int32, shape, 1)


def pair_core(tall):
    number = tall.shape[0]
    split = tall.reshape(number // 2, 2, 8, LANES)
    first, second = split[:, 0], split[:, 1]
    return jnp.where(sublane(first.shape) < 4, turned(first, -2), turned(second, 2))


def quad_low(tall):
    number = tall.shape[0]
    split = tall.reshape(number // 4, 4, 8, LANES)
    at = sublane((number // 4, 8, LANES))
    low = jnp.where(at < 2, split[:, 0], turned(split[:, 1], 2))
    high = jnp.where(at < 6, turned(split[:, 2], 4), turned(split[:, 3], 6))
    return jnp.where(at < 4, low, high)


def pair_edge(tall, quads):
    number = tall.shape[0]
    split = tall.reshape(number // 4, 4, 8, LANES)
    at = sublane(quads.shape)
    even = jnp.where(
        at < 4,
        jnp.where(at < 2, turned(split[:, 0], 2), turned(quads, 2)),
        jnp.where(at < 6, turned(split[:, 1], -2), turned(quads, 4)),
    )
    odd = jnp.where(
        at < 4,
        jnp.where(at < 2, turned(split[:, 2], 2), turned(quads, -2)),
        jnp.where(at < 6, turned(split[:, 3], -2), quads),
    )
    return jnp.stack([even, odd], axis=1).reshape(number // 2, 8, LANES)


def unpair_edge(pairs):
    number = pairs.shape[0]
    split = pairs.reshape(number // 2, 2, 8, LANES)
    first, second = split[:, 0], split[:, 1]
    at = sublane(first.shape)
    near = jnp.where(
        at < 4,
        jnp.where(at < 2, first, turned(first, -2)),
        jnp.where(at < 6, turned(second, 4), turned(second, 2)),
    )
    far = jnp.where(
        at < 4,
        jnp.where(at < 2, turned(first, -2), turned(first, 4)),
        jnp.where(at < 6, turned(second, 2), second),
    )
    return near, far


def join_tall(low, core, near):
    number = low.shape[0]
    split = core.reshape(number, 2, 8, LANES)
    at = sublane(low.shape)
    parts = []
    for y in range(4):
        bottom = turned(low, -2 * y)
        top = turned(near, 6 - 2 * y)
        middle = turned(split[:, y // 2], 2 - 4 * (y % 2))
        parts.append(jnp.where(at < 2, bottom, jnp.where(at < 6, middle, top)))
    return jnp.stack(parts, axis=1).reshape(number * 4, 8, LANES)


def tall_of(ref, x_from, y_from, y_to, size_z=8):
    part = ref[x_from : x_from + SX, y_from * size_z : y_to * size_z, :]
    return part.astype(F32).reshape(-1, 8, LANES)


def rows_of(groups, *lead):
    return groups.reshape(*lead, -1, LANES).astype(BF16)


def as_groups(ref_value):
    return ref_value.astype(F32).reshape(-1, 8, LANES)


def first_kernel(tokens_ref, send_ref, own_ref, low_ref):
    blocks = own_ref.shape[0]
    for block in range(blocks):
        start = SY + block * WY
        for x_from, out_ref in ((SX, send_ref), (0, own_ref)):
            out_ref[block] = rows_of(pair_core(tall_of(tokens_ref, x_from, start, start + WY)))
    size_y = low_ref.shape[1] // SZ
    for x_from in (0, SX):
        low = quad_low(tall_of(tokens_ref, x_from, 0, size_y))
        low_ref[x_from : x_from + SX] = rows_of(low, SX)


def second_kernel(tokens_ref, low_ref, label_ref, send_ref, own_ref, border_ref, inner_ref):
    blocks = own_ref.shape[0]
    size_y = low_ref.shape[1] // SZ

    def edge(x_from, start, stop):
        return pair_edge(
            tall_of(tokens_ref, x_from, start, stop), tall_of(low_ref, x_from, start, stop, SZ)
        )

    for block in range(blocks):
        start = SY + block * WY
        send_ref[block * HALF : (block + 1) * HALF] = rows_of(edge(SX, start, start + WY))
        own_ref[block] = rows_of(edge(0, start, start + WY))
    send_ref[blocks * HALF :] = label_ref[...]
    for half, x_from in enumerate((SX, 0)):
        for start, out_ref in ((0, border_ref), (size_y - SY, inner_ref)):
            stop = start + SY
            out_ref[half, 0] = rows_of(pair_core(tall_of(tokens_ref, x_from, start, stop)))
            out_ref[half, 1] = rows_of(edge(x_from, start, stop))


def third_kernel(inner_ref, border_ref, send_ref, own_ref):
    rows = SY * WZ
    for half, out_ref in enumerate((send_ref, own_ref)):
        for window in range(out_ref.shape[0]):
            for plane in range(SX):
                span = slice(plane * rows, (plane + 1) * rows)
                at = 2 * plane * rows
                out_ref[window, at : at + rows] = inner_ref[half, window, span]
                out_ref[window, at + rows : at + 2 * rows] = border_ref[half, window, span]


def windows_after(x16s, rows, bias_ref, weights, ahead=4):
    gain_attn, gain_mlp, w_qv_t, w_k, w_proj_t, w_up_t, w_down_t = weights
    width = x16s[0].shape[1]
    size = width // HEADS
    scale = size**-0.5 * LOG2E
    eye_window = eye(WTOK)
    eye_width = eye(width)
    n = len(x16s)
    st = []
    for x16, row in zip(x16s, rows):
        x = x16.astype(F32)
        center = x - jnp.mean(x, axis=1, keepdims=True)
        spread = jnp.mean(center * center, axis=1, keepdims=True)
        normed = (center * lax.rsqrt(spread + 1e-05) * gain_attn[...]).astype(BF16)
        x_t = dot_nt(eye_width, x16)
        qv_t = dot_nt(w_qv_t[...], normed).astype(BF16)
        q_t, v_t = qv_t[:width], qv_t[width:]
        k = dot_nn(normed, w_k[...]).astype(BF16)
        column = dot_nt(eye_window, jnp.broadcast_to(row, (WTOK, WTOK)).astype(BF16))
        fade = jnp.where(column == row, 0.0, -1e9 * LOG2E)
        st.append((x_t, q_t, v_t, k, fade))

    tasks = [(w, h) for w in range(n) for h in range(HEADS)]

    def scores(task):
        w, h = task
        x_t, q_t, v_t, k, fade = st[w]
        span = slice(h * size, (h + 1) * size)
        pieces = [jnp.zeros((size, WTOK), BF16)] * HEADS
        pieces[h] = q_t[span]
        return dot_nn(k, jnp.concatenate(pieces, axis=0))

    def attend(task, raw):
        w, h = task
        x_t, q_t, v_t, k, fade = st[w]
        span = slice(h * size, (h + 1) * size)
        score = raw * scale + bias_ref[h] + fade
        weight = jnp.exp2(score - jnp.max(score, axis=0, keepdims=True))
        total = jnp.sum(weight, axis=0, keepdims=True)
        part = dot_nn(v_t[span], weight.astype(BF16))
        return (part * (1.0 / total)).astype(BF16)

    raws = {}
    outs = {}
    for i in range(min(ahead, len(tasks))):
        raws[i] = scores(tasks[i])
    for i, task in enumerate(tasks):
        if i + ahead < len(tasks):
            raws[i + ahead] = scores(tasks[i + ahead])
        outs[task] = attend(task, raws.pop(i))
    middles = []
    for w in range(n):
        attended = jnp.concatenate([outs[(w, h)] for h in range(HEADS)], axis=0)
        middles.append((st[w][0] + dot_nn(w_proj_t[...], attended)).astype(BF16).astype(F32))
    normeds = []
    for middle in middles:
        center = middle - jnp.mean(middle, axis=0, keepdims=True)
        spread = jnp.mean(center * center, axis=0, keepdims=True)
        normeds.append((center * lax.rsqrt(spread + 1e-05) * gain_mlp[...]).astype(BF16))
    hiddens = [dot_nn(w_up_t[...], normed) for normed in normeds]
    hiddens = [gelu(hidden).astype(BF16) for hidden in hiddens]
    afters = [(m + dot_nn(w_down_t[...], h)).astype(BF16) for m, h in zip(middles, hiddens)]
    return [dot_nt(eye_window, after) for after in afters]


def label_row(label_ref, base, window):
    at = base + 2 * window
    pair = label_ref[at : at + 2, :].astype(F32)
    return jnp.concatenate([pair[0:1], pair[1:2]], axis=1)


def inside_kernel(near0_ref, own0_ref, near1_ref, own1_ref, bias_ref, *rest):
    weights, (back_ref, kept_ref) = rest[:7], rest[7:]
    blocks = own0_ref.shape[0]
    x16s, rows = [], []
    for block in range(blocks):
        span = slice(block * HALF, (block + 1) * HALF)
        x16s.append(jnp.concatenate([near0_ref[block], own0_ref[block]], axis=0))
        x16s.append(jnp.concatenate([near1_ref[span], own1_ref[block]], axis=0))
        rows += [label_row(near1_ref, blocks * HALF, 2 * block + layer) for layer in range(2)]
    afters = windows_after(x16s, rows, bias_ref, weights)
    for at, after in enumerate(afters):
        after = after.astype(BF16)
        back_ref[at % 2, at // 2] = after[:HALF]
        kept_ref[at % 2, at // 2] = after[HALF:]


def across_kernel(label_ref, near_ref, own_ref, bias_ref, *rest):
    weights, outs = rest[:7], rest[7:]
    blocks = label_ref.shape[0] // HALF
    x16s = [jnp.concatenate([near_ref[at], own_ref[at]], axis=0) for at in range(2)]
    rows = [label_row(label_ref, blocks * HALF, 2 * blocks + at) for at in range(2)]
    afters = windows_after(x16s, rows, bias_ref, weights)
    for at, after in enumerate(afters):
        split = after.astype(BF16).reshape(2, SX, 2, SY * WZ, LANES)
        for half in range(2):
            for side in range(2):
                outs[2 * half + side][at] = split[half, :, side].reshape(EDGE, LANES)


def far_kernel(
    kept_ref, back_ref, inner_own_ref, inner_back_ref, border_own_ref, border_back_ref, out_ref
):
    blocks = kept_ref.shape[1]
    size_y = out_ref.shape[1] // SZ
    for x_from, whole_ref, inner_ref, border_ref in (
        (0, kept_ref, inner_own_ref, border_own_ref),
        (SX, back_ref, inner_back_ref, border_back_ref),
    ):
        pieces = [(SY + block * WY, WY, whole_ref[1, block]) for block in range(blocks)]
        pieces += [(size_y - SY, SY, inner_ref[1]), (0, SY, border_ref[1])]
        for start, count, piece in pieces:
            far = unpair_edge(as_groups(piece))[1]
            out_ref[x_from : x_from + SX, start * SZ : (start + count) * SZ] = rows_of(far, SX)


def last_kernel(
    low_ref, kept_ref, back_ref, inner_own_ref, inner_back_ref, border_own_ref, border_back_ref, out_ref
):
    blocks = kept_ref.shape[1]
    size_y = low_ref.shape[1] // SZ
    size_z = 8
    for x_from, whole_ref, inner_ref, border_ref in (
        (0, kept_ref, inner_own_ref, border_own_ref),
        (SX, back_ref, inner_back_ref, border_back_ref),
    ):
        pieces = [
            (SY + block * WY, WY, whole_ref[0, block], whole_ref[1, block]) for block in range(blocks)
        ]
        pieces += [(size_y - SY, SY, inner_ref[0], inner_ref[1]), (0, SY, border_ref[0], border_ref[1])]
        for start, count, core, edge in pieces:
            low = tall_of(low_ref, x_from, start, start + count, SZ)
            near = unpair_edge(as_groups(edge))[0]
            tall = join_tall(low, as_groups(core), near)
            out_ref[x_from : x_from + SX, start * size_z : (start + count) * size_z] = rows_of(tall, SX)


def cost(micros):
    return pl.CostEstimate(flops=int(micros * 1.1e9), bytes_accessed=int(micros * 3.3e6), transcendentals=0)


def kernel_call(kernel, name, micros, outs, *operands):
    return pl.pallas_call(
        kernel,
        out_shape=[jax.ShapeDtypeStruct(shape, BF16) for shape in outs],
        cost_estimate=cost(micros),
        compiler_params=pltpu.CompilerParams(vmem_limit_bytes=48 << 20),
        name=name,
    )(*operands)


def per_device(
    tokens, region, rel_index, bias_table, gain_attn, w_qkv, w_proj, gain_mlp, w_up, w_down
):
    size_x, size_y, size_z, width = tokens.shape
    blocks = size_y // WY - 1
    flat = tokens.reshape(size_x, size_y * size_z, width)
    halves = (blocks, HALF, width)
    edges = (2, EDGE, width)
    labels = region.reshape(size_x, size_y // WY, WY, size_z // WZ, WZ).transpose(1, 3, 0, 2, 4)
    labels = labels.reshape(-1, LANES).astype(BF16)

    send0, own0, low = kernel_call(
        first_kernel, "first_pieces", 0.2, [halves, halves, (size_x, size_y * SZ, width)], flat
    )
    near0 = moved(send0, "gx", 1)
    low = moved(low, "gz", -1)
    send1, own1, border, inner = kernel_call(
        second_kernel,
        "second_pieces",
        0.2,
        [(blocks * HALF + labels.shape[0], width), halves, (2,) + edges, (2,) + edges],
        flat,
        low,
        labels,
    )
    near1 = moved(send1, "gx", 1)
    border = moved(border, "gy", -1)
    bias, *turned_weights = prepare(rel_index, bias_table, w_qkv, w_proj, w_up, w_down)
    send2, own2 = kernel_call(
        third_kernel, "third_pieces", 0.2, [(2, HALF, width), (2, HALF, width)], inner, border
    )
    near2 = moved(send2, "gx", 1)
    fixed = (bias, gain_attn[None], gain_mlp[:, None], *turned_weights)
    back, kept = kernel_call(
        inside_kernel, "inside_windows", 5, [(2,) + halves, (2,) + halves], near0, own0, near1, own1, *fixed
    )
    back = moved(back, "gx", -1)
    inner_back, border_back, inner_own, border_own = kernel_call(
        across_kernel, "across_windows", 2.3, [edges] * 4, near1, near2, own2, *fixed
    )
    inner_back = moved(inner_back, "gx", -1)
    border_back = moved(border_back, ("gx", "gy"), (-1, 1))
    border_own = moved(border_own, "gy", 1)
    after = (kept, back, inner_own, inner_back, border_own, border_back)
    far = kernel_call(far_kernel, "far_pieces", 0.1, [(size_x, size_y * SZ, width)], *after)[0]
    far = moved(far, "gz", 1)
    out = kernel_call(last_kernel, "last_pieces", 1, [flat.shape], far, *after)[0]
    return out.reshape(tokens.shape)


def solution(mesh):
    field = P(("cand", "gx"), "gy", "gz", None)
    placed = (field, P(("cand", "gx"), "gy", "gz")) + (P(),) * 8
    return jax.shard_map(
        per_device, mesh=mesh, in_specs=placed, out_specs=field, check_vma=False
    )
```

```python
import math

import jax
import jax.numpy as jnp
from jax import lax
from jax.experimental import pallas as pl
from jax.experimental.pallas import tpu as pltpu
from jax.sharding import PartitionSpec as P

HEADS = 4
WX = 8
WY = 8
WZ = 4
SX = 4
SY = 4
SZ = 2
WTOK = WX * WY * WZ
LANES = 128
F32 = jnp.float32
BF16 = jnp.bfloat16
LOG2E = 1.4426950408889634


def reordered(value):
    run = SY * WZ
    blocks = [
        value[(x * 2 + side) * run : (x * 2 + side + 1) * run] for side in range(2) for x in range(WX)
    ]
    return jnp.concatenate(blocks, axis=0)


def prepare_kernel(
    index_ref, given_ref, w_qkv_ref, w_proj_ref, w_up_ref, w_down_ref, gain_attn_ref, gain_ref,
    bias_ref, gain_attn_out_ref, w_qv_t_ref, w_k_ref, w_proj_t_ref, w_up_t_ref, w_down_t_ref, gain_t_ref, table_ref,
):
    width = w_proj_ref.shape[0]
    w_qv_t_ref[:width] = w_qkv_ref[:, :width].T
    w_qv_t_ref[width:] = w_qkv_ref[:, 2 * width :].T
    w_k_ref[...] = w_qkv_ref[:, width : 2 * width]
    w_proj_t_ref[...] = w_proj_ref[...].T
    w_up_t_ref[...] = w_up_ref[...].T
    w_down_t_ref[...] = w_down_ref[...].T
    gain_attn_out_ref[...] = gain_attn_ref[...]
    gain_t_ref[...] = jnp.broadcast_to(gain_ref[...], (LANES, width)).T
    rows = given_ref.shape[1]
    table_ref[:, :rows] = given_ref[...]
    chunks = table_ref.shape[1] // LANES
    index = reordered(reordered(index_ref[...].astype(F32)).T).astype(jnp.int32)
    for column in range(0, WTOK, LANES):
        for row in range(0, WTOK, 8):
            part = index[row : row + 8, column : column + LANES]
            low = part & (LANES - 1)
            high = part >> 7
            found = [jnp.zeros((8, LANES), F32) for _ in range(HEADS)]
            for chunk in range(chunks):
                here = high == chunk
                for head in range(HEADS):
                    span = slice(chunk * LANES, (chunk + 1) * LANES)
                    line = jnp.broadcast_to(table_ref[head : head + 1, span], (8, LANES))
                    got = jnp.take_along_axis(line, low, axis=1, mode="promise_in_bounds")
                    found[head] = jnp.where(here, got, found[head])
            for head in range(HEADS):
                bias_ref[head, row : row + 8, column : column + LANES] = found[head] * LOG2E


def prepare(rel_index, table, w_qkv, w_proj, w_up, w_down, gain_attn, gain_mlp):
    width, hidden = w_up.shape
    shapes = [(2 * width, width), (width, width), (width, width), (hidden, width), (width, hidden)]
    return pl.pallas_call(
        prepare_kernel,
        out_shape=[jax.ShapeDtypeStruct((HEADS, WTOK, WTOK), F32), jax.ShapeDtypeStruct((1, width), F32)]
        + [jax.ShapeDtypeStruct(shape, BF16) for shape in shapes]
        + [jax.ShapeDtypeStruct((width, LANES), F32)],
        scratch_shapes=[pltpu.VMEM((HEADS, -(-table.shape[1] // LANES) * LANES), F32)],
        cost_estimate=cost(1),
        compiler_params=pltpu.CompilerParams(vmem_limit_bytes=32 << 20),
        name="bias_and_weights",
    )(rel_index, table, w_qkv, w_proj, w_up, w_down, gain_attn, gain_mlp)


def cost(micros):
    return pl.CostEstimate(
        flops=int(micros * 1.1e9), bytes_accessed=int(micros * 3.3e6), transcendentals=0
    )


def dot_nn(left, right):
    return lax.dot_general(left, right, (((1,), (0,)), ((), ())), preferred_element_type=F32)


def dot_nt(left, right):
    return lax.dot_general(left, right, (((1,), (1,)), ((), ())), preferred_element_type=F32)


def eye(size):
    rows = lax.broadcasted_iota(jnp.int32, (size, size), 0)
    columns = lax.broadcasted_iota(jnp.int32, (size, size), 1)
    return (rows == columns).astype(BF16)


def gelu(value):
    return 0.5 * value * (1.0 + lax.erf(value * (0.5**0.5)))


HALF = SX * WY * WZ
QUARTER = HALF // 2


def moved(value, axis, steps):
    names = (axis,) if isinstance(axis, str) else tuple(axis)
    moves = (steps,) if isinstance(axis, str) else tuple(steps)
    counts = [lax.axis_size(name) for name in names]
    pairs = []
    for source in range(math.prod(counts)):
        left, target, stride = source, 0, 1
        for count, move in zip(reversed(counts), reversed(moves)):
            target += (left % count + move) % count * stride
            left //= count
            stride *= count
        pairs.append((source, target))
    return lax.ppermute(value, names, pairs)


def turned(value, steps):
    return pltpu.roll(value, steps % 8, axis=1)


def sublane(shape):
    return lax.broadcasted_iota(jnp.int32, shape, 1)


def pair_core(tall):
    number = tall.shape[0]
    split = tall.reshape(number // 2, 2, 8, LANES)
    first, second = split[:, 0], split[:, 1]
    return jnp.where(sublane(first.shape) < 4, turned(first, -2), turned(second, 2))


def quad_low(tall):
    number = tall.shape[0]
    split = tall.reshape(number // 4, 4, 8, LANES)
    at = sublane((number // 4, 8, LANES))
    low = jnp.where(at < 2, split[:, 0], turned(split[:, 1], 2))
    high = jnp.where(at < 6, turned(split[:, 2], 4), turned(split[:, 3], 6))
    return jnp.where(at < 4, low, high)


def pair_edge(tall, quads):
    number = tall.shape[0]
    split = tall.reshape(number // 4, 4, 8, LANES)
    at = sublane(quads.shape)
    even = jnp.where(
        at < 4,
        jnp.where(at < 2, turned(split[:, 0], 2), turned(quads, 2)),
        jnp.where(at < 6, turned(split[:, 1], -2), turned(quads, 4)),
    )
    odd = jnp.where(
        at < 4,
        jnp.where(at < 2, turned(split[:, 2], 2), turned(quads, -2)),
        jnp.where(at < 6, turned(split[:, 3], -2), quads),
    )
    return jnp.stack([even, odd], axis=1).reshape(number // 2, 8, LANES)


def unpair_edge(pairs):
    number = pairs.shape[0]
    split = pairs.reshape(number // 2, 2, 8, LANES)
    first, second = split[:, 0], split[:, 1]
    at = sublane(first.shape)
    near = jnp.where(
        at < 4,
        jnp.where(at < 2, first, turned(first, -2)),
        jnp.where(at < 6, turned(second, 4), turned(second, 2)),
    )
    far = jnp.where(
        at < 4,
        jnp.where(at < 2, turned(first, -2), turned(first, 4)),
        jnp.where(at < 6, turned(second, 2), second),
    )
    return near, far


def join_tall(low, core, near):
    number = low.shape[0]
    split = core.reshape(number, 2, 8, LANES)
    at = sublane(low.shape)
    parts = []
    for y in range(4):
        bottom = turned(low, -2 * y)
        top = turned(near, 6 - 2 * y)
        middle = turned(split[:, y // 2], 2 - 4 * (y % 2))
        parts.append(jnp.where(at < 2, bottom, jnp.where(at < 6, middle, top)))
    return jnp.stack(parts, axis=1).reshape(number * 4, 8, LANES)


def tall_of(ref, x_from, y_from, y_to, size_z=8):
    part = ref[x_from : x_from + SX, y_from * size_z : y_to * size_z, :]
    return part.astype(F32).reshape(-1, 8, LANES)


def rows_of(groups, *lead):
    return groups.reshape(*lead, -1, LANES).astype(BF16)


def as_groups(ref_value):
    return ref_value.astype(F32).reshape(-1, 8, LANES)


def low_kernel(tokens_ref, low_ref):
    size_y = low_ref.shape[1] // SZ
    for x_from in (0, SX):
        low = quad_low(tall_of(tokens_ref, x_from, 0, size_y))
        low_ref[x_from : x_from + SX] = rows_of(low, SX)


def shifted_kernel(tokens_ref, low_ref, region_ref, send_ref, own_ref, send_y_ref, own_y_ref):
    windows = own_ref.shape[0]
    size_y = low_ref.shape[1] // SZ

    def core(x_from, start):
        return rows_of(pair_core(tall_of(tokens_ref, x_from, start, start + SY)))

    def edge(x_from, start):
        return rows_of(
            pair_edge(
                tall_of(tokens_ref, x_from, start, start + SY),
                tall_of(low_ref, x_from, start, start + SY, SZ),
            )
        )

    for at in range(windows):
        piece = (core, edge)[at % 2]
        for side in range(2):
            start = SY + at // 2 * WY + side * SY
            row = at * HALF + side * QUARTER
            send_ref[row : row + QUARTER] = piece(SX, start)
            own_ref[at, side * QUARTER : (side + 1) * QUARTER] = piece(0, start)
    for strip, start in enumerate((0, size_y - SY)):
        for half, x_from in enumerate((SX, 0)):
            for layer, piece in enumerate((core, edge)):
                row = ((strip * 2 + half) * 2 + layer) * QUARTER
                rows = piece(x_from, start)
                send_y_ref[row : row + QUARTER] = rows
                own_y_ref[row : row + QUARTER] = rows
    labels = region_ref[...].astype(F32).reshape(-1, size_y)
    blank = jnp.zeros((labels.shape[0], LANES - size_y), F32)
    labels = jnp.concatenate([labels, blank], axis=1).astype(BF16)
    send_ref[windows * HALF :] = labels
    send_y_ref[8 * QUARTER :] = labels


def across_pieces_kernel(own_ref, got_ref, send_ref):
    strip = 2 * QUARTER
    send_ref[:strip] = own_ref[2 * strip : 3 * strip]
    send_ref[strip : 2 * strip] = got_ref[:strip]
    send_ref[2 * strip : 3 * strip] = got_ref[2 * strip : 3 * strip]
    send_ref[3 * strip : 4 * strip] = own_ref[:strip]
    send_ref[4 * strip :] = got_ref[4 * strip :]


def windows_after(x16s, labels, spans, bias_ref, weights, ahead=4):
    gain_attn, w_qv_t, w_k, w_proj_t, w_up_t, w_down_t, gain_mlp = weights
    width = x16s[0].shape[1]
    size = width // HEADS
    scale = size**-0.5 * LOG2E
    eye_window = eye(WTOK)
    eye_width = eye(width)
    gain_mlp = jnp.concatenate([gain_mlp[...]] * (WTOK // LANES), axis=1)
    states = []
    for x16, (column, row), span in zip(x16s, labels, spans):
        x = x16.astype(F32)
        center = x - jnp.mean(x, axis=1, keepdims=True)
        spread = jnp.mean(center * center, axis=1, keepdims=True)
        normed = (center * lax.rsqrt(spread + 1e-05) * gain_attn[...]).astype(BF16)
        x_t = dot_nt(eye_width, x16[span])
        if span == slice(0, WTOK):
            qv_t = dot_nt(w_qv_t[...], normed).astype(BF16)
            q_t, v_t = qv_t[:width], qv_t[width:]
        else:
            q_t = dot_nt(w_qv_t[:width], normed[span]).astype(BF16)
            v_t = dot_nt(w_qv_t[width:], normed).astype(BF16)
        k = dot_nn(normed, w_k[...]).astype(BF16)
        fade = jnp.where(column[:, span] == row[:, span], 0.0, -1e9 * LOG2E)
        states.append((x_t, q_t, v_t, k, fade, span))
    tasks = [(at, head) for at in range(len(states)) for head in range(HEADS)]

    def scores(task):
        at, head = task
        _, q_t, _, k, _, _ = states[at]
        pieces = [jnp.zeros((size, q_t.shape[1]), BF16)] * HEADS
        pieces[head] = q_t[head * size : (head + 1) * size]
        return dot_nn(k, jnp.concatenate(pieces, axis=0))

    def attend(task, raw):
        at, head = task
        _, _, v_t, _, fade, span = states[at]
        score = raw * scale + bias_ref[head, :, span] + fade
        weight = jnp.exp2(score - jnp.max(score, axis=0, keepdims=True))
        total = jnp.sum(weight, axis=0, keepdims=True)
        part = dot_nn(v_t[head * size : (head + 1) * size], weight.astype(BF16))
        return (part * (1.0 / total)).astype(BF16)

    raws, parts = {}, {}
    for at in range(min(ahead, len(tasks))):
        raws[at] = scores(tasks[at])
    for at, task in enumerate(tasks):
        if at + ahead < len(tasks):
            raws[at + ahead] = scores(tasks[at + ahead])
        parts[task] = attend(task, raws.pop(at))
    attended = [
        jnp.concatenate([parts[at, head] for head in range(HEADS)], axis=0)
        for at in range(len(states))
    ]
    residual = [state[0] for state in states]
    joined = WTOK // residual[0].shape[1]
    if joined > 1:
        group = lambda values: [
            jnp.concatenate(values[at : at + joined], axis=1) for at in range(0, len(values), joined)
        ]
        attended, residual = group(attended), group(residual)
    middles = [
        (x_t + dot_nn(w_proj_t[...], value)).astype(BF16).astype(F32)
        for x_t, value in zip(residual, attended)
    ]
    normeds = []
    for middle in middles:
        center = middle - jnp.mean(middle, axis=0, keepdims=True)
        spread = jnp.mean(center * center, axis=0, keepdims=True)
        normeds.append((center * lax.rsqrt(spread + 1e-05) * gain_mlp).astype(BF16))
    hiddens = [dot_nn(w_up_t[...], normed) for normed in normeds]
    hiddens = [gelu(hidden).astype(BF16) for hidden in hiddens]
    afters = [
        (middle + dot_nn(w_down_t[...], hidden)).astype(BF16)
        for middle, hidden in zip(middles, hiddens)
    ]
    return [dot_nt(eye_window, after).astype(BF16) for after in afters]


def window_labels(region, number):
    at = lax.broadcasted_iota(jnp.int32, (WTOK, region.shape[0]), 0)
    line = lax.broadcasted_iota(jnp.int32, (WTOK, region.shape[0]), 1)
    wanted = (at % HALF) // (SY * WZ) * 8 + (number % 2) * WZ + at % WZ
    lines = dot_nn((line == wanted).astype(BF16), region)
    at = lax.broadcasted_iota(jnp.int32, lines.shape, 0)
    y = lax.broadcasted_iota(jnp.int32, lines.shape, 1)
    wanted = number // 2 * WY + at // HALF * SY + at // WZ % SY
    lone = jnp.where(y == wanted, lines, 0.0).astype(BF16)
    ones = jnp.ones((WTOK, lines.shape[1]), BF16)
    return dot_nt(lone, ones), dot_nt(ones[:8], lone)[:1]


def quarters(rows, start):
    at = start * QUARTER
    return rows[at : at + QUARTER]


def inside_kernel(near_ref, own_ref, bias_ref, *rest):
    weights, (back_ref, kept_ref) = rest[:7], rest[7:]
    windows = own_ref.shape[0]
    region = near_ref[windows * HALF :]
    x16s = []
    for at in range(windows):
        near, own = near_ref[at * HALF : (at + 1) * HALF], own_ref[at]
        x16s.append(
            jnp.concatenate([near[:QUARTER], own[:QUARTER], near[QUARTER:], own[QUARTER:]], axis=0)
        )
    labels = [window_labels(region, at) for at in range(windows)]
    afters = windows_after(x16s, labels, [slice(0, WTOK)] * windows, bias_ref, weights)
    for at, after in enumerate(afters):
        for side in range(2):
            back_ref[at % 2, at // 2, side] = quarters(after, 2 * side)
            kept_ref[at % 2, at // 2, side] = quarters(after, 2 * side + 1)


def across_kernel(inside_ref, near_ref, own_ref, got_ref, bias_ref, *rest):
    weights, (back_ref, kept_ref) = rest[:7], rest[7:]
    size = near_ref.shape[0] - 8 * QUARTER
    windows = (inside_ref.shape[0] - size) // HALF
    x16s, labels, spans = [], [], []
    for place in range(2):
        region = (inside_ref[windows * HALF :], near_ref[8 * QUARTER :])[place]
        for layer in range(2):
            near = [quarters(near_ref, 4 * place + 2 * side + layer) for side in range(2)]
            if place == 0:
                own = [quarters(own_ref, 6 + layer), quarters(got_ref, 2 + layer)]
            else:
                own = [quarters(got_ref, 6 + layer), quarters(own_ref, 2 + layer)]
            x16s.append(jnp.concatenate([near[0], own[0], near[1], own[1]], axis=0))
            labels.append(window_labels(region, windows + layer))
            spans.append(slice(place * HALF, (place + 1) * HALF))
    afters = windows_after(x16s, labels, spans, bias_ref, weights)
    for place, after in enumerate(afters):
        for layer in range(2):
            back_ref[layer, place] = quarters(after, 2 * layer)
            kept_ref[layer, place] = quarters(after, 2 * layer + 1)


def strips(size_y, inside_ref, across_ref):
    blocks = inside_ref.shape[1]
    for block in range(blocks):
        for side in range(2):
            yield SY + block * WY + side * SY, [inside_ref[layer, block, side] for layer in range(2)]
    yield size_y - SY, [across_ref[layer, 0] for layer in range(2)]
    yield 0, [across_ref[layer, 1] for layer in range(2)]


def far_kernel(kept_ref, back_ref, kept_across_ref, back_across_ref, out_ref):
    size_y = out_ref.shape[1] // SZ
    for x_from, inside_ref, across_ref in (
        (0, kept_ref, kept_across_ref),
        (SX, back_ref, back_across_ref),
    ):
        for start, (_, edge) in strips(size_y, inside_ref, across_ref):
            far = unpair_edge(as_groups(edge))[1]
            out_ref[x_from : x_from + SX, start * SZ : (start + SY) * SZ] = rows_of(far, SX)


def last_kernel(low_ref, kept_ref, back_ref, kept_across_ref, back_across_ref, out_ref):
    size_y = low_ref.shape[1] // SZ
    size_z = 8
    for x_from, inside_ref, across_ref in (
        (0, kept_ref, kept_across_ref),
        (SX, back_ref, back_across_ref),
    ):
        for start, (core, edge) in strips(size_y, inside_ref, across_ref):
            low = tall_of(low_ref, x_from, start, start + SY, SZ)
            near = unpair_edge(as_groups(edge))[0]
            tall = join_tall(low, as_groups(core), near)
            out_ref[x_from : x_from + SX, start * size_z : (start + SY) * size_z] = rows_of(tall, SX)


def kernel_call(kernel, name, micros, outs, *operands):
    return pl.pallas_call(
        kernel,
        out_shape=[jax.ShapeDtypeStruct(shape, BF16) for shape in outs],
        cost_estimate=cost(micros),
        compiler_params=pltpu.CompilerParams(vmem_limit_bytes=48 << 20),
        name=name,
    )(*operands)


def per_device(
    tokens, region, rel_index, bias_table, gain_attn, w_qkv, w_proj, gain_mlp, w_up, w_down
):
    size_x, size_y, size_z, width = tokens.shape
    windows = 2 * (size_y // WY - 1)
    lines = size_x * size_z
    flat = tokens.reshape(size_x, size_y * size_z, width)
    low = kernel_call(low_kernel, "low_pieces", 0.2, [(size_x, size_y * SZ, width)], flat)[0]
    low = moved(low, "gz", -1)
    sent, own, strip, own_strip = kernel_call(
        shifted_kernel,
        "shifted_pieces",
        0.3,
        [
            (windows * HALF + lines, width),
            (windows, HALF, width),
            (8 * QUARTER + lines, width),
            (8 * QUARTER, width),
        ],
        flat,
        low,
        region.transpose(0, 2, 1),
    )
    near = moved(sent, "gx", 1)
    if lax.axis_size("gy") == 2:
        got = moved(strip, "gy", 1)
    else:
        got = jnp.concatenate(
            [moved(strip[: 4 * QUARTER], "gy", -1), moved(strip[4 * QUARTER :], "gy", 1)]
        )
    fixed = prepare(
        rel_index, bias_table.T, w_qkv, w_proj, w_up, w_down, gain_attn[None], gain_mlp[None]
    )
    sent_across = kernel_call(
        across_pieces_kernel, "across_pieces", 0.2, [(8 * QUARTER + lines, width)], own_strip, got
    )[0]
    near_across = moved(sent_across, "gx", 1)
    halves = (2, windows // 2, 2, QUARTER, width)
    back, kept = kernel_call(
        inside_kernel, "inside_windows", 15, [halves, halves], near, own, *fixed
    )
    back = moved(back, "gx", -1)
    halves = (2, 2, QUARTER, width)
    back_across, kept_across = kernel_call(
        across_kernel, "across_windows", 2.3, [halves, halves], near, near_across, own_strip, got, *fixed
    )
    back_across = moved(back_across, "gx", -1)
    after = (kept, back, kept_across, back_across)
    far = kernel_call(far_kernel, "far_pieces", 0.1, [(size_x, size_y * SZ, width)], *after)[0]
    far = moved(far, "gz", 1)
    out = kernel_call(last_kernel, "last_pieces", 1, [flat.shape], far, *after)[0]
    return out.reshape(tokens.shape)


def solution(mesh):
    field = P(("cand", "gx"), "gy", "gz", None)
    placed = (field, P(("cand", "gx"), "gy", "gz")) + (P(),) * 8
    return jax.shard_map(
        per_device, mesh=mesh, in_specs=placed, out_specs=field, check_vma=False
    )
```

```python
import math

import jax
import jax.numpy as jnp
from jax import lax
from jax.experimental import pallas as pl
from jax.experimental.pallas import tpu as pltpu
from jax.sharding import PartitionSpec as P

HEADS = 4
WX = 8
WY = 8
WZ = 4
SX = 4
SY = 4
SZ = 2
WTOK = WX * WY * WZ
LANES = 128
F32 = jnp.float32
BF16 = jnp.bfloat16
LOG2E = 1.4426950408889634


def reordered(value):
    run = SY * WZ
    blocks = [
        value[(x * 2 + side) * run : (x * 2 + side + 1) * run] for side in range(2) for x in range(WX)
    ]
    return jnp.concatenate(blocks, axis=0)


def weights_kernel(
    _, w_qkv_ref, w_proj_ref, w_up_ref, w_down_ref, gain_attn_ref, gain_ref,
    gain_attn_out_ref, w_qv_t_ref, w_k_ref, w_proj_t_ref, w_up_t_ref, w_down_t_ref, gain_t_ref,
):
    width = w_proj_ref.shape[0]
    w_qv_t_ref[:width] = w_qkv_ref[:, :width].T
    w_qv_t_ref[width:] = w_qkv_ref[:, 2 * width :].T
    w_k_ref[...] = w_qkv_ref[:, width : 2 * width]
    w_proj_t_ref[...] = w_proj_ref[...].T
    w_up_t_ref[...] = w_up_ref[...].T
    w_down_t_ref[...] = w_down_ref[...].T
    gain_attn_out_ref[...] = gain_attn_ref[...]
    gain_t_ref[...] = jnp.broadcast_to(gain_ref[...], (LANES, width)).T


def bias_kernel(index_ref, given_ref, bias_ref, table_ref):
    rows = given_ref.shape[1]
    table_ref[:, :rows] = given_ref[...]
    chunks = table_ref.shape[1] // LANES
    index = reordered(reordered(index_ref[...].astype(F32)).T).astype(jnp.int32)
    for column in range(0, WTOK, LANES):
        for row in range(0, WTOK, 8):
            part = index[row : row + 8, column : column + LANES]
            low = part & (LANES - 1)
            high = part >> 7
            found = [jnp.zeros((8, LANES), F32) for _ in range(HEADS)]
            for chunk in range(chunks):
                here = high == chunk
                for head in range(HEADS):
                    span = slice(chunk * LANES, (chunk + 1) * LANES)
                    line = jnp.broadcast_to(table_ref[head : head + 1, span], (8, LANES))
                    got = jnp.take_along_axis(line, low, axis=1, mode="promise_in_bounds")
                    found[head] = jnp.where(here, got, found[head])
            for head in range(HEADS):
                bias_ref[head, row : row + 8, column : column + LANES] = found[head] * LOG2E


def prepare(rel_index, table, w_qkv, w_proj, w_up, w_down, gain_attn, gain_mlp):
    width, hidden = w_up.shape
    bias = pl.pallas_call(
        bias_kernel,
        out_shape=jax.ShapeDtypeStruct((HEADS, WTOK, WTOK), F32),
        scratch_shapes=[pltpu.VMEM((HEADS, -(-table.shape[1] // LANES) * LANES), F32)],
        cost_estimate=cost(1),
        compiler_params=pltpu.CompilerParams(vmem_limit_bytes=32 << 20),
        name="gather_bias",
    )(rel_index, table)
    shapes = [(2 * width, width), (width, width), (width, width), (hidden, width), (width, hidden)]
    others = pl.pallas_call(
        weights_kernel,
        in_specs=[pl.BlockSpec(memory_space=pl.ANY)] + [pl.BlockSpec(memory_space=pltpu.VMEM)] * 6,
        out_shape=[jax.ShapeDtypeStruct((1, width), F32)]
        + [jax.ShapeDtypeStruct(shape, BF16) for shape in shapes]
        + [jax.ShapeDtypeStruct((width, LANES), F32)],
        cost_estimate=cost(0.3),
        compiler_params=pltpu.CompilerParams(vmem_limit_bytes=32 << 20),
        name="turn_weights",
    )(bias, w_qkv, w_proj, w_up, w_down, gain_attn, gain_mlp)
    return bias, *others


def cost(micros):
    return pl.CostEstimate(
        flops=int(micros * 1.1e9), bytes_accessed=int(micros * 3.3e6), transcendentals=0
    )


def dot_nn(left, right):
    return lax.dot_general(left, right, (((1,), (0,)), ((), ())), preferred_element_type=F32)


def dot_nt(left, right):
    return lax.dot_general(left, right, (((1,), (1,)), ((), ())), preferred_element_type=F32)


def eye(size):
    rows = lax.broadcasted_iota(jnp.int32, (size, size), 0)
    columns = lax.broadcasted_iota(jnp.int32, (size, size), 1)
    return (rows == columns).astype(BF16)


def gelu(value):
    return 0.5 * value * (1.0 + lax.erf(value * (0.5**0.5)))


HALF = SX * WY * WZ
QUARTER = HALF // 2


def moved(value, axis, steps):
    names = (axis,) if isinstance(axis, str) else tuple(axis)
    moves = (steps,) if isinstance(axis, str) else tuple(steps)
    counts = [lax.axis_size(name) for name in names]
    pairs = []
    for source in range(math.prod(counts)):
        left, target, stride = source, 0, 1
        for count, move in zip(reversed(counts), reversed(moves)):
            target += (left % count + move) % count * stride
            left //= count
            stride *= count
        pairs.append((source, target))
    return lax.ppermute(value, names, pairs)


def turned(value, steps):
    return pltpu.roll(value, steps % 8, axis=1)


def sublane(shape):
    return lax.broadcasted_iota(jnp.int32, shape, 1)


def pair_core(tall):
    number = tall.shape[0]
    split = tall.reshape(number // 2, 2, 8, LANES)
    first, second = split[:, 0], split[:, 1]
    return jnp.where(sublane(first.shape) < 4, turned(first, -2), turned(second, 2))


def quad_low(tall):
    number = tall.shape[0]
    split = tall.reshape(number // 4, 4, 8, LANES)
    at = sublane((number // 4, 8, LANES))
    low = jnp.where(at < 2, split[:, 0], turned(split[:, 1], 2))
    high = jnp.where(at < 6, turned(split[:, 2], 4), turned(split[:, 3], 6))
    return jnp.where(at < 4, low, high)


def pair_edge(tall, quads):
    number = tall.shape[0]
    split = tall.reshape(number // 4, 4, 8, LANES)
    at = sublane(quads.shape)
    even = jnp.where(
        at < 4,
        jnp.where(at < 2, turned(split[:, 0], 2), turned(quads, 2)),
        jnp.where(at < 6, turned(split[:, 1], -2), turned(quads, 4)),
    )
    odd = jnp.where(
        at < 4,
        jnp.where(at < 2, turned(split[:, 2], 2), turned(quads, -2)),
        jnp.where(at < 6, turned(split[:, 3], -2), quads),
    )
    return jnp.stack([even, odd], axis=1).reshape(number // 2, 8, LANES)


def unpair_edge(pairs):
    number = pairs.shape[0]
    split = pairs.reshape(number // 2, 2, 8, LANES)
    first, second = split[:, 0], split[:, 1]
    at = sublane(first.shape)
    near = jnp.where(
        at < 4,
        jnp.where(at < 2, first, turned(first, -2)),
        jnp.where(at < 6, turned(second, 4), turned(second, 2)),
    )
    far = jnp.where(
        at < 4,
        jnp.where(at < 2, turned(first, -2), turned(first, 4)),
        jnp.where(at < 6, turned(second, 2), second),
    )
    return near, far


def join_tall(low, core, near):
    number = low.shape[0]
    split = core.reshape(number, 2, 8, LANES)
    at = sublane(low.shape)
    parts = []
    for y in range(4):
        bottom = turned(low, -2 * y)
        top = turned(near, 6 - 2 * y)
        middle = turned(split[:, y // 2], 2 - 4 * (y % 2))
        parts.append(jnp.where(at < 2, bottom, jnp.where(at < 6, middle, top)))
    return jnp.stack(parts, axis=1).reshape(number * 4, 8, LANES)


def tall_of(ref, x_from, y_from, y_to, size_z=8):
    part = ref[x_from : x_from + SX, y_from * size_z : y_to * size_z, :]
    return part.astype(F32).reshape(-1, 8, LANES)


def rows_of(groups, *lead):
    return groups.reshape(*lead, -1, LANES).astype(BF16)


def as_groups(ref_value):
    return ref_value.astype(F32).reshape(-1, 8, LANES)


def low_kernel(tokens_ref, low_ref):
    size_y = low_ref.shape[1] // SZ
    for x_from in (0, SX):
        low = quad_low(tall_of(tokens_ref, x_from, 0, size_y))
        low_ref[x_from : x_from + SX] = rows_of(low, SX)


def shifted_kernel(
    tokens_ref, low_ref, region_ref, given_ref, send_ref, own_ref, send_y_ref, own_y_ref, table_ref
):
    table_ref[...] = given_ref[...]
    windows = own_ref.shape[0]
    size_y = low_ref.shape[1] // SZ

    def core(x_from, start):
        return rows_of(pair_core(tall_of(tokens_ref, x_from, start, start + SY)))

    def edge(x_from, start):
        return rows_of(
            pair_edge(
                tall_of(tokens_ref, x_from, start, start + SY),
                tall_of(low_ref, x_from, start, start + SY, SZ),
            )
        )

    for at in range(windows):
        piece = (core, edge)[at % 2]
        for side in range(2):
            start = SY + at // 2 * WY + side * SY
            row = at * HALF + side * QUARTER
            send_ref[row : row + QUARTER] = piece(SX, start)
            own_ref[at, side * QUARTER : (side + 1) * QUARTER] = piece(0, start)
    for strip, start in enumerate((0, size_y - SY)):
        for half, x_from in enumerate((SX, 0)):
            for layer, piece in enumerate((core, edge)):
                row = ((strip * 2 + half) * 2 + layer) * QUARTER
                rows = piece(x_from, start)
                send_y_ref[row : row + QUARTER] = rows
                own_y_ref[row : row + QUARTER] = rows
    labels = region_ref[...].astype(F32).reshape(-1, size_y)
    blank = jnp.zeros((labels.shape[0], LANES - size_y), F32)
    labels = jnp.concatenate([labels, blank], axis=1).astype(BF16)
    send_ref[windows * HALF :] = labels
    send_y_ref[8 * QUARTER :] = labels


def across_pieces_kernel(own_ref, got_ref, send_ref):
    strip = 2 * QUARTER
    send_ref[:strip] = own_ref[2 * strip : 3 * strip]
    send_ref[strip : 2 * strip] = got_ref[:strip]
    send_ref[2 * strip : 3 * strip] = got_ref[2 * strip : 3 * strip]
    send_ref[3 * strip : 4 * strip] = own_ref[:strip]
    send_ref[4 * strip :] = got_ref[4 * strip :]


def windows_after(x16s, labels, spans, bias_ref, weights, ahead=4):
    gain_attn, w_qv_t, w_k, w_proj_t, w_up_t, w_down_t, gain_mlp = weights
    width = x16s[0].shape[1]
    size = width // HEADS
    scale = size**-0.5 * LOG2E
    eye_window = eye(WTOK)
    eye_width = eye(width)
    gain_mlp = jnp.concatenate([gain_mlp[...]] * (WTOK // LANES), axis=1)
    states = []
    for x16, (column, row), span in zip(x16s, labels, spans):
        x = x16.astype(F32)
        center = x - jnp.mean(x, axis=1, keepdims=True)
        spread = jnp.mean(center * center, axis=1, keepdims=True)
        normed = (center * lax.rsqrt(spread + 1e-05) * gain_attn[...]).astype(BF16)
        x_t = dot_nt(eye_width, x16[span])
        if span == slice(0, WTOK):
            qv_t = dot_nt(w_qv_t[...], normed).astype(BF16)
            q_t, v_t = qv_t[:width], qv_t[width:]
        else:
            q_t = dot_nt(w_qv_t[:width], normed[span]).astype(BF16)
            v_t = dot_nt(w_qv_t[width:], normed).astype(BF16)
        k = dot_nn(normed, w_k[...]).astype(BF16)
        lane = lax.broadcasted_iota(jnp.int32, column.shape, 1).astype(F32)
        k = jnp.concatenate([k, jnp.where(column == lane, 1.0, 0.0).astype(BF16)], axis=1)
        line = lax.broadcasted_iota(jnp.int32, (LANES, q_t.shape[1]), 0).astype(F32)
        fade = jnp.where(row[:, span] == line, 0.0, -1e10).astype(BF16)
        states.append((x_t, q_t, v_t, k, fade, span))
    tasks = [(at, head) for at in range(len(states)) for head in range(HEADS)]

    def scores(task):
        at, head = task
        _, q_t, _, k, fade, _ = states[at]
        pieces = [jnp.zeros((size, q_t.shape[1]), BF16)] * HEADS
        pieces[head] = q_t[head * size : (head + 1) * size]
        return dot_nn(k, jnp.concatenate(pieces + [fade], axis=0))

    def attend(task, raw):
        at, head = task
        _, _, v_t, _, _, span = states[at]
        score = raw * scale + bias_ref[head, :, span]
        weight = jnp.exp2(score - jnp.max(score, axis=0, keepdims=True))
        total = jnp.sum(weight, axis=0, keepdims=True)
        part = dot_nn(v_t[head * size : (head + 1) * size], weight.astype(BF16))
        return (part * (1.0 / total)).astype(BF16)

    raws, parts = {}, {}
    for at in range(min(ahead, len(tasks))):
        raws[at] = scores(tasks[at])
    for at, task in enumerate(tasks):
        if at + ahead < len(tasks):
            raws[at + ahead] = scores(tasks[at + ahead])
        parts[task] = attend(task, raws.pop(at))
    attended = [
        jnp.concatenate([parts[at, head] for head in range(HEADS)], axis=0)
        for at in range(len(states))
    ]
    residual = [state[0] for state in states]
    joined = WTOK // residual[0].shape[1]
    if joined > 1:
        group = lambda values: [
            jnp.concatenate(values[at : at + joined], axis=1) for at in range(0, len(values), joined)
        ]
        attended, residual = group(attended), group(residual)
    middles = [
        (x_t + dot_nn(w_proj_t[...], value)).astype(BF16).astype(F32)
        for x_t, value in zip(residual, attended)
    ]
    normeds = []
    for middle in middles:
        center = middle - jnp.mean(middle, axis=0, keepdims=True)
        spread = jnp.mean(center * center, axis=0, keepdims=True)
        normeds.append((center * lax.rsqrt(spread + 1e-05) * gain_mlp).astype(BF16))
    hiddens = [dot_nn(w_up_t[...], normed) for normed in normeds]
    hiddens = [gelu(hidden).astype(BF16) for hidden in hiddens]
    afters = [
        (middle + dot_nn(w_down_t[...], hidden)).astype(BF16)
        for middle, hidden in zip(middles, hiddens)
    ]
    return [dot_nt(eye_window, after).astype(BF16) for after in afters]


def window_labels(region, number):
    at = lax.broadcasted_iota(jnp.int32, (WTOK, region.shape[0]), 0)
    line = lax.broadcasted_iota(jnp.int32, (WTOK, region.shape[0]), 1)
    wanted = (at % HALF) // (SY * WZ) * 8 + (number % 2) * WZ + at % WZ
    lines = dot_nn((line == wanted).astype(BF16), region)
    at = lax.broadcasted_iota(jnp.int32, lines.shape, 0)
    y = lax.broadcasted_iota(jnp.int32, lines.shape, 1)
    wanted = number // 2 * WY + at // HALF * SY + at // WZ % SY
    lone = jnp.where(y == wanted, lines, 0.0).astype(BF16)
    ones = jnp.ones((LANES, lines.shape[1]), BF16)
    return dot_nt(lone, ones), dot_nt(ones[:8], lone)[:1]


def quarters(rows, start):
    at = start * QUARTER
    return rows[at : at + QUARTER]


def inside_kernel(near_ref, own_ref, bias_ref, *rest):
    weights, (back_ref, kept_ref) = rest[:7], rest[7:]
    windows = own_ref.shape[0]
    region = near_ref[windows * HALF :]
    x16s = []
    for at in range(windows):
        near, own = near_ref[at * HALF : (at + 1) * HALF], own_ref[at]
        x16s.append(
            jnp.concatenate([near[:QUARTER], own[:QUARTER], near[QUARTER:], own[QUARTER:]], axis=0)
        )
    labels = [window_labels(region, at) for at in range(windows)]
    afters = windows_after(x16s, labels, [slice(0, WTOK)] * windows, bias_ref, weights)
    for at, after in enumerate(afters):
        for side in range(2):
            back_ref[at % 2, at // 2, side] = quarters(after, 2 * side)
            kept_ref[at % 2, at // 2, side] = quarters(after, 2 * side + 1)


def across_kernel(inside_ref, near_ref, own_ref, got_ref, bias_ref, *rest):
    weights, (back_ref, kept_ref) = rest[:7], rest[7:]
    size = near_ref.shape[0] - 8 * QUARTER
    windows = (inside_ref.shape[0] - size) // HALF
    x16s, labels, spans = [], [], []
    for place in range(2):
        region = (inside_ref[windows * HALF :], near_ref[8 * QUARTER :])[place]
        for layer in range(2):
            near = [quarters(near_ref, 4 * place + 2 * side + layer) for side in range(2)]
            if place == 0:
                own = [quarters(own_ref, 6 + layer), quarters(got_ref, 2 + layer)]
            else:
                own = [quarters(got_ref, 6 + layer), quarters(own_ref, 2 + layer)]
            x16s.append(jnp.concatenate([near[0], own[0], near[1], own[1]], axis=0))
            labels.append(window_labels(region, windows + layer))
            spans.append(slice(place * HALF, (place + 1) * HALF))
    afters = windows_after(x16s, labels, spans, bias_ref, weights, ahead=8)
    for place, after in enumerate(afters):
        for layer in range(2):
            back_ref[layer, place] = quarters(after, 2 * layer)
            kept_ref[layer, place] = quarters(after, 2 * layer + 1)


def strips(size_y, inside_ref, across_ref):
    blocks = inside_ref.shape[1]
    for block in range(blocks):
        for side in range(2):
            yield SY + block * WY + side * SY, [inside_ref[layer, block, side] for layer in range(2)]
    yield size_y - SY, [across_ref[layer, 0] for layer in range(2)]
    yield 0, [across_ref[layer, 1] for layer in range(2)]


def far_kernel(kept_ref, back_ref, kept_across_ref, back_across_ref, out_ref):
    size_y = out_ref.shape[1] // SZ
    for x_from, inside_ref, across_ref in (
        (0, kept_ref, kept_across_ref),
        (SX, back_ref, back_across_ref),
    ):
        for start, (_, edge) in strips(size_y, inside_ref, across_ref):
            far = unpair_edge(as_groups(edge))[1]
            out_ref[x_from : x_from + SX, start * SZ : (start + SY) * SZ] = rows_of(far, SX)


def last_kernel(
    low_ref, kept_ref, back_ref, kept_across_ref, back_across_ref, out_ref, block_ref, sent
):
    size_y = low_ref.shape[1] // SZ
    size_z = 8
    moves = []
    for x_from, inside_ref, across_ref in (
        (0, kept_ref, kept_across_ref),
        (SX, back_ref, back_across_ref),
    ):
        planes = slice(x_from, x_from + SX)
        for start, (core, edge) in strips(size_y, inside_ref, across_ref):
            low = tall_of(low_ref, x_from, start, start + SY, SZ)
            near = unpair_edge(as_groups(edge))[0]
            tall = join_tall(low, as_groups(core), near)
            block_ref[planes, start * size_z : (start + SY) * size_z] = rows_of(tall, SX)
        move = pltpu.make_async_copy(
            block_ref.at[planes], out_ref.at[planes], sent.at[len(moves)]
        )
        move.start()
        moves.append(move)
    for move in moves:
        move.wait()


def last_call(low, after, shape):
    return pl.pallas_call(
        last_kernel,
        in_specs=[pl.BlockSpec(memory_space=pltpu.VMEM)] * 5,
        out_specs=pl.BlockSpec(memory_space=pl.ANY),
        out_shape=jax.ShapeDtypeStruct(shape, BF16),
        scratch_shapes=[pltpu.VMEM(shape, BF16), pltpu.SemaphoreType.DMA((2,))],
        cost_estimate=cost(1),
        compiler_params=pltpu.CompilerParams(vmem_limit_bytes=48 << 20),
        name="last_pieces",
    )(low, *after)


def kernel_call(kernel, name, micros, outs, *operands):
    return pl.pallas_call(
        kernel,
        out_shape=[
            shape if hasattr(shape, "dtype") else jax.ShapeDtypeStruct(shape, BF16) for shape in outs
        ],
        cost_estimate=cost(micros),
        compiler_params=pltpu.CompilerParams(vmem_limit_bytes=48 << 20),
        name=name,
    )(*operands)


def per_device(
    tokens, region, rel_index, bias_table, gain_attn, w_qkv, w_proj, gain_mlp, w_up, w_down
):
    size_x, size_y, size_z, width = tokens.shape
    windows = 2 * (size_y // WY - 1)
    lines = size_x * size_z
    flat = tokens.reshape(size_x, size_y * size_z, width)
    low = kernel_call(low_kernel, "low_pieces", 0.2, [(size_x, size_y * SZ, width)], flat)[0]
    low = moved(low, "gz", -1)
    sent, own, strip, own_strip, table = kernel_call(
        shifted_kernel,
        "shifted_pieces",
        0.3,
        [
            (windows * HALF + lines, width),
            (windows, HALF, width),
            (8 * QUARTER + lines, width),
            (8 * QUARTER, width),
            jax.ShapeDtypeStruct(bias_table.shape[::-1], F32),
        ],
        flat,
        low,
        region.transpose(0, 2, 1),
        bias_table.T,
    )
    near = moved(sent, "gx", 1)
    if lax.axis_size("gy") == 2:
        got = moved(strip, "gy", 1)
    else:
        got = jnp.concatenate(
            [moved(strip[: 4 * QUARTER], "gy", -1), moved(strip[4 * QUARTER :], "gy", 1)]
        )
    fixed = prepare(
        rel_index, table, w_qkv, w_proj, w_up, w_down, gain_attn[None], gain_mlp[None]
    )
    sent_across = kernel_call(
        across_pieces_kernel, "across_pieces", 0.2, [(8 * QUARTER + lines, width)], own_strip, got
    )[0]
    near_across = moved(sent_across, "gx", 1)
    halves = (2, windows // 2, 2, QUARTER, width)
    back, kept = kernel_call(
        inside_kernel, "inside_windows", 15, [halves, halves], near, own, *fixed
    )
    back = moved(back, "gx", -1)
    halves = (2, 2, QUARTER, width)
    back_across, kept_across = kernel_call(
        across_kernel, "across_windows", 2.3, [halves, halves], near, near_across, own_strip, got, *fixed
    )
    back_across = moved(back_across, "gx", -1)
    after = (kept, back, kept_across, back_across)
    far = kernel_call(far_kernel, "far_pieces", 0.1, [(size_x, size_y * SZ, width)], *after)[0]
    far = moved(far, "gz", 1)
    return last_call(far, after, flat.shape).reshape(tokens.shape)


def solution(mesh):
    field = P(("cand", "gx"), "gy", "gz", None)
    placed = (field, P(("cand", "gx"), "gy", "gz")) + (P(),) * 8
    return jax.shard_map(
        per_device, mesh=mesh, in_specs=placed, out_specs=field, check_vma=False
    )
```

```python
import math

import jax
import jax.numpy as jnp
from jax import lax
from jax.experimental import pallas as pl
from jax.experimental.pallas import tpu as pltpu
from jax.sharding import PartitionSpec as P

HEADS = 4
WX = 8
WY = 8
WZ = 4
SX = 4
SY = 4
SZ = 2
WTOK = WX * WY * WZ
LANES = 128
F32 = jnp.float32
BF16 = jnp.bfloat16
LOG2E = 1.4426950408889634


def reordered(value):
    run = SY * WZ
    blocks = [
        value[(x * 2 + side) * run : (x * 2 + side + 1) * run] for side in range(2) for x in range(WX)
    ]
    return jnp.concatenate(blocks, axis=0)


def weights_kernel(
    _, w_qkv_ref, w_proj_ref, w_up_ref, w_down_ref, gain_attn_ref, gain_ref,
    gain_attn_out_ref, w_qv_t_ref, w_k_ref, w_proj_t_ref, w_up_t_ref, w_down_t_ref, gain_t_ref,
):
    width = w_proj_ref.shape[0]
    w_qv_t_ref[:width] = w_qkv_ref[:, :width].T
    w_qv_t_ref[width:] = w_qkv_ref[:, 2 * width :].T
    w_k_ref[...] = w_qkv_ref[:, width : 2 * width]
    w_proj_t_ref[...] = w_proj_ref[...].T
    w_up_t_ref[...] = w_up_ref[...].T
    w_down_t_ref[...] = w_down_ref[...].T
    gain_attn_out_ref[...] = gain_attn_ref[...]
    gain_t_ref[...] = jnp.broadcast_to(gain_ref[...], (LANES, width)).T


def gather_rows(index_ref, table_ref, bias_ref, start):
    chunks = table_ref.shape[1] // LANES
    for column in range(0, WTOK, LANES):
        for row in range(0, bias_ref.shape[1], 8):
            part = index_ref[start + row : start + row + 8, column : column + LANES]
            low = part & (LANES - 1)
            high = part >> 7
            found = [jnp.zeros((8, LANES), F32) for _ in range(HEADS)]
            for chunk in range(chunks):
                here = high == chunk
                for head in range(HEADS):
                    span = slice(chunk * LANES, (chunk + 1) * LANES)
                    line = jnp.broadcast_to(table_ref[head : head + 1, span], (8, LANES))
                    got = jnp.take_along_axis(line, low, axis=1, mode="promise_in_bounds")
                    found[head] = jnp.where(here, got, found[head])
            for head in range(HEADS):
                bias_ref[head, row : row + 8, column : column + LANES] = found[head] * LOG2E


def first_bias_kernel(
    given_index_ref, given_ref, region_ref, gain_ref, other_gain_ref,
    bias_ref, index_ref, table_ref, region_out_ref, gain_out_ref, other_gain_out_ref,
):
    region_out_ref[...] = region_ref[...]
    gain_out_ref[...] = gain_ref[...]
    other_gain_out_ref[...] = other_gain_ref[...]
    rows = given_ref.shape[1]
    table_ref[...] = jnp.zeros_like(table_ref)
    table_ref[:, :rows] = given_ref[...]
    index = reordered(reordered(given_index_ref[...].astype(F32)).T)
    index_ref[...] = index.astype(jnp.int32)
    gather_rows(index_ref, table_ref, bias_ref, 0)


def second_bias_kernel(index_ref, table_ref, bias_ref):
    gather_rows(index_ref, table_ref, bias_ref, WTOK - bias_ref.shape[1])


def first_bias(rel_index, table, region, gain_attn, gain_mlp):
    passed = (region, gain_attn, gain_mlp)
    padded = -(-table.shape[1] // LANES) * LANES
    return pl.pallas_call(
        first_bias_kernel,
        out_shape=[
            jax.ShapeDtypeStruct((HEADS, EARLY, WTOK), F32),
            jax.ShapeDtypeStruct((WTOK, WTOK), jnp.int32),
            jax.ShapeDtypeStruct((HEADS, padded), F32),
        ]
        + [jax.ShapeDtypeStruct(a.shape, a.dtype) for a in passed],
        cost_estimate=cost(0.7),
        compiler_params=pltpu.CompilerParams(vmem_limit_bytes=32 << 20),
        name="first_bias",
    )(rel_index, table, *passed)


def second_bias(index, table):
    return pl.pallas_call(
        second_bias_kernel,
        out_shape=jax.ShapeDtypeStruct((HEADS, WTOK - EARLY, WTOK), F32),
        cost_estimate=cost(1),
        compiler_params=pltpu.CompilerParams(vmem_limit_bytes=32 << 20),
        name="second_bias",
    )(index, table)


def turn_weights(after, w_qkv, w_proj, w_up, w_down, gain_attn, gain_mlp):
    width, hidden = w_up.shape
    shapes = [(2 * width, width), (width, width), (width, width), (hidden, width), (width, hidden)]
    return pl.pallas_call(
        weights_kernel,
        in_specs=[pl.BlockSpec(memory_space=pl.ANY)] + [pl.BlockSpec(memory_space=pltpu.VMEM)] * 6,
        out_shape=[jax.ShapeDtypeStruct((1, width), F32)]
        + [jax.ShapeDtypeStruct(shape, BF16) for shape in shapes]
        + [jax.ShapeDtypeStruct((width, LANES), F32)],
        cost_estimate=cost(0.3),
        compiler_params=pltpu.CompilerParams(vmem_limit_bytes=32 << 20),
        name="turn_weights",
    )(after, w_qkv, w_proj, w_up, w_down, gain_attn, gain_mlp)


def cost(micros):
    return pl.CostEstimate(
        flops=int(micros * 1.1e9), bytes_accessed=int(micros * 3.3e6), transcendentals=0
    )


def dot_nn(left, right):
    return lax.dot_general(left, right, (((1,), (0,)), ((), ())), preferred_element_type=F32)


def dot_nt(left, right):
    return lax.dot_general(left, right, (((1,), (1,)), ((), ())), preferred_element_type=F32)


def eye(size):
    rows = lax.broadcasted_iota(jnp.int32, (size, size), 0)
    columns = lax.broadcasted_iota(jnp.int32, (size, size), 1)
    return (rows == columns).astype(BF16)


def gelu(value):
    return 0.5 * value * (1.0 + lax.erf(value * (0.5**0.5)))


HALF = SX * WY * WZ
QUARTER = HALF // 2
EARLY = 32


def moved(value, axis, steps):
    names = (axis,) if isinstance(axis, str) else tuple(axis)
    moves = (steps,) if isinstance(axis, str) else tuple(steps)
    counts = [lax.axis_size(name) for name in names]
    pairs = []
    for source in range(math.prod(counts)):
        left, target, stride = source, 0, 1
        for count, move in zip(reversed(counts), reversed(moves)):
            target += (left % count + move) % count * stride
            left //= count
            stride *= count
        pairs.append((source, target))
    return lax.ppermute(value, names, pairs)


def turned(value, steps):
    return pltpu.roll(value, steps % 8, axis=1)


def sublane(shape):
    return lax.broadcasted_iota(jnp.int32, shape, 1)


def pair_core(tall):
    number = tall.shape[0]
    split = tall.reshape(number // 2, 2, 8, LANES)
    first, second = split[:, 0], split[:, 1]
    return jnp.where(sublane(first.shape) < 4, turned(first, -2), turned(second, 2))


def quad_low(tall):
    number = tall.shape[0]
    split = tall.reshape(number // 4, 4, 8, LANES)
    at = sublane((number // 4, 8, LANES))
    low = jnp.where(at < 2, split[:, 0], turned(split[:, 1], 2))
    high = jnp.where(at < 6, turned(split[:, 2], 4), turned(split[:, 3], 6))
    return jnp.where(at < 4, low, high)


def pair_edge(tall, quads):
    number = tall.shape[0]
    split = tall.reshape(number // 4, 4, 8, LANES)
    at = sublane(quads.shape)
    even = jnp.where(
        at < 4,
        jnp.where(at < 2, turned(split[:, 0], 2), turned(quads, 2)),
        jnp.where(at < 6, turned(split[:, 1], -2), turned(quads, 4)),
    )
    odd = jnp.where(
        at < 4,
        jnp.where(at < 2, turned(split[:, 2], 2), turned(quads, -2)),
        jnp.where(at < 6, turned(split[:, 3], -2), quads),
    )
    return jnp.stack([even, odd], axis=1).reshape(number // 2, 8, LANES)


def unpair_edge(pairs):
    number = pairs.shape[0]
    split = pairs.reshape(number // 2, 2, 8, LANES)
    first, second = split[:, 0], split[:, 1]
    at = sublane(first.shape)
    near = jnp.where(
        at < 4,
        jnp.where(at < 2, first, turned(first, -2)),
        jnp.where(at < 6, turned(second, 4), turned(second, 2)),
    )
    far = jnp.where(
        at < 4,
        jnp.where(at < 2, turned(first, -2), turned(first, 4)),
        jnp.where(at < 6, turned(second, 2), second),
    )
    return near, far


def join_tall(low, core, near):
    number = low.shape[0]
    split = core.reshape(number, 2, 8, LANES)
    at = sublane(low.shape)
    parts = []
    for y in range(4):
        bottom = turned(low, -2 * y)
        top = turned(near, 6 - 2 * y)
        middle = turned(split[:, y // 2], 2 - 4 * (y % 2))
        parts.append(jnp.where(at < 2, bottom, jnp.where(at < 6, middle, top)))
    return jnp.stack(parts, axis=1).reshape(number * 4, 8, LANES)


def tall_of(ref, x_from, y_from, y_to, size_z=8):
    part = ref[x_from : x_from + SX, y_from * size_z : y_to * size_z, :]
    return part.astype(F32).reshape(-1, 8, LANES)


def rows_of(groups, *lead):
    return groups.reshape(*lead, -1, LANES).astype(BF16)


def as_groups(ref_value):
    return ref_value.astype(F32).reshape(-1, 8, LANES)


def low_kernel(tokens_ref, low_ref):
    size_y = low_ref.shape[1] // SZ
    for x_from in (0, SX):
        low = quad_low(tall_of(tokens_ref, x_from, 0, size_y))
        low_ref[x_from : x_from + SX] = rows_of(low, SX)


def shifted_kernel(
    tokens_ref, low_ref, region_ref, send_ref, own_ref, send_y_ref, own_y_ref
):
    windows = own_ref.shape[0]
    size_y = low_ref.shape[1] // SZ

    def core(x_from, start):
        return rows_of(pair_core(tall_of(tokens_ref, x_from, start, start + SY)))

    def edge(x_from, start):
        return rows_of(
            pair_edge(
                tall_of(tokens_ref, x_from, start, start + SY),
                tall_of(low_ref, x_from, start, start + SY, SZ),
            )
        )

    for at in range(windows):
        piece = (core, edge)[at % 2]
        for side in range(2):
            start = SY + at // 2 * WY + side * SY
            row = at * HALF + side * QUARTER
            send_ref[row : row + QUARTER] = piece(SX, start)
            own_ref[at, side * QUARTER : (side + 1) * QUARTER] = piece(0, start)
    for strip, start in enumerate((0, size_y - SY)):
        for half, x_from in enumerate((SX, 0)):
            for layer, piece in enumerate((core, edge)):
                row = ((strip * 2 + half) * 2 + layer) * QUARTER
                rows = piece(x_from, start)
                send_y_ref[row : row + QUARTER] = rows
                own_y_ref[row : row + QUARTER] = rows
    labels = region_ref[...].astype(F32).reshape(-1, size_y)
    blank = jnp.zeros((labels.shape[0], LANES - size_y), F32)
    labels = jnp.concatenate([labels, blank], axis=1).astype(BF16)
    send_ref[windows * HALF :] = labels
    send_y_ref[8 * QUARTER :] = labels


def across_pieces_kernel(own_ref, got_ref, send_ref):
    strip = 2 * QUARTER
    send_ref[:strip] = own_ref[2 * strip : 3 * strip]
    send_ref[strip : 2 * strip] = got_ref[:strip]
    send_ref[2 * strip : 3 * strip] = got_ref[2 * strip : 3 * strip]
    send_ref[3 * strip : 4 * strip] = own_ref[:strip]
    send_ref[4 * strip :] = got_ref[4 * strip :]


def windows_after(x16s, labels, spans, bias_refs, weights, ahead=4):
    gain_attn, w_qv_t, w_k, w_proj_t, w_up_t, w_down_t, gain_mlp = weights
    width = x16s[0].shape[1]
    size = width // HEADS
    scale = size**-0.5 * LOG2E
    eye_window = eye(WTOK)
    eye_width = eye(width)
    gain_mlp = jnp.concatenate([gain_mlp[...]] * (WTOK // LANES), axis=1)
    states = []
    for x16, (column, row), span in zip(x16s, labels, spans):
        x = x16.astype(F32)
        center = x - jnp.mean(x, axis=1, keepdims=True)
        spread = jnp.mean(center * center, axis=1, keepdims=True)
        normed = (center * lax.rsqrt(spread + 1e-05) * gain_attn[...]).astype(BF16)
        x_t = dot_nt(eye_width, x16[span])
        if span == slice(0, WTOK):
            qv_t = dot_nt(w_qv_t[...], normed).astype(BF16)
            q_t, v_t = qv_t[:width], qv_t[width:]
        else:
            q_t = dot_nt(w_qv_t[:width], normed[span]).astype(BF16)
            v_t = dot_nt(w_qv_t[width:], normed).astype(BF16)
        k = dot_nn(normed, w_k[...]).astype(BF16)
        lane = lax.broadcasted_iota(jnp.int32, column.shape, 1).astype(F32)
        k = jnp.concatenate([k, jnp.where(column == lane, 1.0, 0.0).astype(BF16)], axis=1)
        line = lax.broadcasted_iota(jnp.int32, (LANES, q_t.shape[1]), 0).astype(F32)
        fade = jnp.where(row[:, span] == line, 0.0, -1e10).astype(BF16)
        states.append((x_t, q_t, v_t, k, fade, span))
    tasks = [(at, head) for at in range(len(states)) for head in range(HEADS)]

    def scores(task):
        at, head = task
        _, q_t, _, k, fade, _ = states[at]
        pieces = [jnp.zeros((size, q_t.shape[1]), BF16)] * HEADS
        pieces[head] = q_t[head * size : (head + 1) * size]
        return dot_nn(k, jnp.concatenate(pieces + [fade], axis=0))

    def attend(task, raw):
        at, head = task
        _, _, v_t, _, _, span = states[at]
        bias = jnp.concatenate([ref[head, :, span] for ref in bias_refs], axis=0)
        score = raw * scale + bias
        weight = jnp.exp2(score - jnp.max(score, axis=0, keepdims=True))
        total = jnp.sum(weight, axis=0, keepdims=True)
        part = dot_nn(v_t[head * size : (head + 1) * size], weight.astype(BF16))
        return (part * (1.0 / total)).astype(BF16)

    raws, parts = {}, {}
    for at in range(min(ahead, len(tasks))):
        raws[at] = scores(tasks[at])
    for at, task in enumerate(tasks):
        if at + ahead < len(tasks):
            raws[at + ahead] = scores(tasks[at + ahead])
        parts[task] = attend(task, raws.pop(at))
    attended = [
        jnp.concatenate([parts[at, head] for head in range(HEADS)], axis=0)
        for at in range(len(states))
    ]
    residual = [state[0] for state in states]
    joined = WTOK // residual[0].shape[1]
    if joined > 1:
        group = lambda values: [
            jnp.concatenate(values[at : at + joined], axis=1) for at in range(0, len(values), joined)
        ]
        attended, residual = group(attended), group(residual)
    middles = [
        (x_t + dot_nn(w_proj_t[...], value)).astype(BF16).astype(F32)
        for x_t, value in zip(residual, attended)
    ]
    normeds = []
    for middle in middles:
        center = middle - jnp.mean(middle, axis=0, keepdims=True)
        spread = jnp.mean(center * center, axis=0, keepdims=True)
        normeds.append((center * lax.rsqrt(spread + 1e-05) * gain_mlp).astype(BF16))
    hiddens = [dot_nn(w_up_t[...], normed) for normed in normeds]
    hiddens = [gelu(hidden).astype(BF16) for hidden in hiddens]
    afters = [
        (middle + dot_nn(w_down_t[...], hidden)).astype(BF16)
        for middle, hidden in zip(middles, hiddens)
    ]
    return [dot_nt(eye_window, after).astype(BF16) for after in afters]


def window_labels(region, number):
    at = lax.broadcasted_iota(jnp.int32, (WTOK, region.shape[0]), 0)
    line = lax.broadcasted_iota(jnp.int32, (WTOK, region.shape[0]), 1)
    wanted = (at % HALF) // (SY * WZ) * 8 + (number % 2) * WZ + at % WZ
    lines = dot_nn((line == wanted).astype(BF16), region)
    at = lax.broadcasted_iota(jnp.int32, lines.shape, 0)
    y = lax.broadcasted_iota(jnp.int32, lines.shape, 1)
    wanted = number // 2 * WY + at // HALF * SY + at // WZ % SY
    lone = jnp.where(y == wanted, lines, 0.0).astype(BF16)
    ones = jnp.ones((LANES, lines.shape[1]), BF16)
    return dot_nt(lone, ones), dot_nt(ones[:8], lone)[:1]


def quarters(rows, start):
    at = start * QUARTER
    return rows[at : at + QUARTER]


def inside_kernel(near_ref, own_ref, early_ref, late_ref, *rest):
    weights, (back_ref, kept_ref) = rest[:7], rest[7:]
    windows = own_ref.shape[0]
    region = near_ref[windows * HALF :]
    x16s = []
    for at in range(windows):
        near, own = near_ref[at * HALF : (at + 1) * HALF], own_ref[at]
        x16s.append(
            jnp.concatenate([near[:QUARTER], own[:QUARTER], near[QUARTER:], own[QUARTER:]], axis=0)
        )
    labels = [window_labels(region, at) for at in range(windows)]
    afters = windows_after(x16s, labels, [slice(0, WTOK)] * windows, (early_ref, late_ref), weights)
    for at, after in enumerate(afters):
        for side in range(2):
            back_ref[at % 2, at // 2, side] = quarters(after, 2 * side)
            kept_ref[at % 2, at // 2, side] = quarters(after, 2 * side + 1)


def across_kernel(inside_ref, near_ref, own_ref, got_ref, early_ref, late_ref, *rest):
    weights, (back_ref, kept_ref) = rest[:7], rest[7:]
    size = near_ref.shape[0] - 8 * QUARTER
    windows = (inside_ref.shape[0] - size) // HALF
    x16s, labels, spans = [], [], []
    for place in range(2):
        region = (inside_ref[windows * HALF :], near_ref[8 * QUARTER :])[place]
        for layer in range(2):
            near = [quarters(near_ref, 4 * place + 2 * side + layer) for side in range(2)]
            if place == 0:
                own = [quarters(own_ref, 6 + layer), quarters(got_ref, 2 + layer)]
            else:
                own = [quarters(got_ref, 6 + layer), quarters(own_ref, 2 + layer)]
            x16s.append(jnp.concatenate([near[0], own[0], near[1], own[1]], axis=0))
            labels.append(window_labels(region, windows + layer))
            spans.append(slice(place * HALF, (place + 1) * HALF))
    afters = windows_after(x16s, labels, spans, (early_ref, late_ref), weights, ahead=8)
    for place, after in enumerate(afters):
        for layer in range(2):
            back_ref[layer, place] = quarters(after, 2 * layer)
            kept_ref[layer, place] = quarters(after, 2 * layer + 1)


def strips(size_y, inside_ref, across_ref):
    blocks = inside_ref.shape[1]
    for block in range(blocks):
        for side in range(2):
            yield SY + block * WY + side * SY, [inside_ref[layer, block, side] for layer in range(2)]
    yield size_y - SY, [across_ref[layer, 0] for layer in range(2)]
    yield 0, [across_ref[layer, 1] for layer in range(2)]


def far_kernel(kept_ref, back_ref, kept_across_ref, back_across_ref, out_ref):
    size_y = out_ref.shape[1] // SZ
    for x_from, inside_ref, across_ref in (
        (0, kept_ref, kept_across_ref),
        (SX, back_ref, back_across_ref),
    ):
        for start, (_, edge) in strips(size_y, inside_ref, across_ref):
            far = unpair_edge(as_groups(edge))[1]
            out_ref[x_from : x_from + SX, start * SZ : (start + SY) * SZ] = rows_of(far, SX)


def last_kernel(
    low_ref, kept_ref, back_ref, kept_across_ref, back_across_ref, out_ref, block_ref, sent
):
    size_y = low_ref.shape[1] // SZ
    size_z = 8
    moves = []
    for x_from, inside_ref, across_ref in (
        (0, kept_ref, kept_across_ref),
        (SX, back_ref, back_across_ref),
    ):
        planes = slice(x_from, x_from + SX)
        for start, (core, edge) in strips(size_y, inside_ref, across_ref):
            low = tall_of(low_ref, x_from, start, start + SY, SZ)
            near = unpair_edge(as_groups(edge))[0]
            tall = join_tall(low, as_groups(core), near)
            block_ref[planes, start * size_z : (start + SY) * size_z] = rows_of(tall, SX)
        move = pltpu.make_async_copy(
            block_ref.at[planes], out_ref.at[planes], sent.at[len(moves)]
        )
        move.start()
        moves.append(move)
    for move in moves:
        move.wait()


def last_call(low, after, shape):
    return pl.pallas_call(
        last_kernel,
        in_specs=[pl.BlockSpec(memory_space=pltpu.VMEM)] * 5,
        out_specs=pl.BlockSpec(memory_space=pl.ANY),
        out_shape=jax.ShapeDtypeStruct(shape, BF16),
        scratch_shapes=[pltpu.VMEM(shape, BF16), pltpu.SemaphoreType.DMA((2,))],
        cost_estimate=cost(1),
        compiler_params=pltpu.CompilerParams(vmem_limit_bytes=48 << 20),
        name="last_pieces",
    )(low, *after)


def kernel_call(kernel, name, micros, outs, *operands):
    return pl.pallas_call(
        kernel,
        out_shape=[
            shape if hasattr(shape, "dtype") else jax.ShapeDtypeStruct(shape, BF16) for shape in outs
        ],
        cost_estimate=cost(micros),
        compiler_params=pltpu.CompilerParams(vmem_limit_bytes=48 << 20),
        name=name,
    )(*operands)


def per_device(
    tokens, region, rel_index, bias_table, gain_attn, w_qkv, w_proj, gain_mlp, w_up, w_down
):
    size_x, size_y, size_z, width = tokens.shape
    windows = 2 * (size_y // WY - 1)
    lines = size_x * size_z
    flat = tokens.reshape(size_x, size_y * size_z, width)
    low = kernel_call(low_kernel, "low_pieces", 0.2, [(size_x, size_y * SZ, width)], flat)[0]
    low = moved(low, "gz", -1)
    early, index, table, region, gain_attn, gain_mlp = first_bias(
        rel_index, bias_table.T, region.transpose(0, 2, 1), gain_attn[None], gain_mlp[None]
    )
    sent, own, strip, own_strip = kernel_call(
        shifted_kernel,
        "shifted_pieces",
        0.3,
        [
            (windows * HALF + lines, width),
            (windows, HALF, width),
            (8 * QUARTER + lines, width),
            (8 * QUARTER, width),
        ],
        flat,
        low,
        region,
    )
    near = moved(sent, "gx", 1)
    if lax.axis_size("gy") == 2:
        got = moved(strip, "gy", 1)
    else:
        got = jnp.concatenate(
            [moved(strip[: 4 * QUARTER], "gy", -1), moved(strip[4 * QUARTER :], "gy", 1)]
        )
    late = second_bias(index, table)
    fixed = (
        early, late, *turn_weights(late, w_qkv, w_proj, w_up, w_down, gain_attn, gain_mlp)
    )
    sent_across = kernel_call(
        across_pieces_kernel, "across_pieces", 0.2, [(8 * QUARTER + lines, width)], own_strip, got
    )[0]
    near_across = moved(sent_across, "gx", 1)
    halves = (2, windows // 2, 2, QUARTER, width)
    back, kept = kernel_call(
        inside_kernel, "inside_windows", 15, [halves, halves], near, own, *fixed
    )
    back = moved(back, "gx", -1)
    halves = (2, 2, QUARTER, width)
    back_across, kept_across = kernel_call(
        across_kernel, "across_windows", 2.3, [halves, halves], near, near_across, own_strip, got, *fixed
    )
    back_across = moved(back_across, "gx", -1)
    after = (kept, back, kept_across, back_across)
    far = kernel_call(far_kernel, "far_pieces", 0.1, [(size_x, size_y * SZ, width)], *after)[0]
    far = moved(far, "gz", 1)
    return last_call(far, after, flat.shape).reshape(tokens.shape)


def solution(mesh):
    field = P(("cand", "gx"), "gy", "gz", None)
    placed = (field, P(("cand", "gx"), "gy", "gz")) + (P(),) * 8
    return jax.shard_map(
        per_device, mesh=mesh, in_specs=placed, out_specs=field, check_vma=False
    )
```

```python
import functools
import math

import jax
import jax.numpy as jnp
from jax import lax
from jax.experimental import pallas as pl
from jax.experimental.pallas import tpu as pltpu
from jax.sharding import PartitionSpec as P

HEADS = 4
WX = 8
WY = 8
WZ = 4
SX = 4
SY = 4
SZ = 2
WTOK = WX * WY * WZ
LANES = 128
F32 = jnp.float32
BF16 = jnp.bfloat16
LOG2E = 1.4426950408889634


def reordered(value):
    run = SY * WZ
    blocks = [
        value[(x * 2 + side) * run : (x * 2 + side + 1) * run] for side in range(2) for x in range(WX)
    ]
    return jnp.concatenate(blocks, axis=0)


def weights_kernel(
    _, w_qkv_ref, w_proj_ref, w_up_ref, w_down_ref, gain_attn_ref, gain_ref,
    gain_attn_out_ref, w_qv_t_ref, w_k_ref, w_proj_t_ref, w_up_t_ref, w_down_t_ref, gain_t_ref,
):
    width = w_proj_ref.shape[0]
    w_qv_t_ref[:width] = w_qkv_ref[:, :width].T
    w_qv_t_ref[width:] = w_qkv_ref[:, 2 * width :].T
    w_k_ref[...] = w_qkv_ref[:, width : 2 * width]
    w_proj_t_ref[...] = w_proj_ref[...].T
    w_up_t_ref[...] = w_up_ref[...].T
    w_down_t_ref[...] = w_down_ref[...].T
    gain_attn_out_ref[...] = gain_attn_ref[...]
    gain_t_ref[...] = jnp.broadcast_to(gain_ref[...], (LANES, width)).T


def gather_rows(index_ref, table_ref, bias_ref, start):
    chunks = table_ref.shape[1] // LANES
    for column in range(0, WTOK, LANES):
        for row in range(0, bias_ref.shape[1], 8):
            part = index_ref[start + row : start + row + 8, column : column + LANES]
            low = part & (LANES - 1)
            high = part >> 7
            found = [jnp.zeros((8, LANES), F32) for _ in range(HEADS)]
            for chunk in range(chunks):
                here = high == chunk
                for head in range(HEADS):
                    span = slice(chunk * LANES, (chunk + 1) * LANES)
                    line = jnp.broadcast_to(table_ref[head : head + 1, span], (8, LANES))
                    got = jnp.take_along_axis(line, low, axis=1, mode="promise_in_bounds")
                    found[head] = jnp.where(here, got, found[head])
            for head in range(HEADS):
                bias_ref[head, row : row + 8, column : column + LANES] = found[head] * LOG2E


def first_bias_kernel(
    given_index_ref, given_ref, region_ref, gain_ref, other_gain_ref,
    bias_ref, index_ref, table_ref, region_out_ref, gain_out_ref, other_gain_out_ref,
):
    region_out_ref[...] = region_ref[...]
    gain_out_ref[...] = gain_ref[...]
    other_gain_out_ref[...] = other_gain_ref[...]
    rows = given_ref.shape[1]
    table_ref[...] = jnp.zeros_like(table_ref)
    table_ref[:, :rows] = given_ref[...]
    index = reordered(reordered(given_index_ref[...].astype(F32)).T)
    index_ref[...] = index.astype(jnp.int32)
    gather_rows(index_ref, table_ref, bias_ref, 0)


def second_bias_kernel(index_ref, table_ref, bias_ref):
    gather_rows(index_ref, table_ref, bias_ref, WTOK - bias_ref.shape[1])


def first_bias(rel_index, table, region, gain_attn, gain_mlp):
    passed = (region, gain_attn, gain_mlp)
    padded = -(-table.shape[1] // LANES) * LANES
    return pl.pallas_call(
        first_bias_kernel,
        out_shape=[
            jax.ShapeDtypeStruct((HEADS, EARLY, WTOK), F32),
            jax.ShapeDtypeStruct((WTOK, WTOK), jnp.int32),
            jax.ShapeDtypeStruct((HEADS, padded), F32),
        ]
        + [jax.ShapeDtypeStruct(a.shape, a.dtype) for a in passed],
        cost_estimate=cost(0.7),
        compiler_params=pltpu.CompilerParams(vmem_limit_bytes=32 << 20),
        name="first_bias",
    )(rel_index, table, *passed)


def second_bias(index, table):
    return pl.pallas_call(
        second_bias_kernel,
        out_shape=jax.ShapeDtypeStruct((HEADS, WTOK - EARLY, WTOK), F32),
        cost_estimate=cost(1),
        compiler_params=pltpu.CompilerParams(vmem_limit_bytes=32 << 20),
        name="second_bias",
    )(index, table)


def turn_weights(after, w_qkv, w_proj, w_up, w_down, gain_attn, gain_mlp):
    width, hidden = w_up.shape
    shapes = [(2 * width, width), (width, width), (width, width), (hidden, width), (width, hidden)]
    return pl.pallas_call(
        weights_kernel,
        in_specs=[pl.BlockSpec(memory_space=pl.ANY)] + [pl.BlockSpec(memory_space=pltpu.VMEM)] * 6,
        out_shape=[jax.ShapeDtypeStruct((1, width), F32)]
        + [jax.ShapeDtypeStruct(shape, BF16) for shape in shapes]
        + [jax.ShapeDtypeStruct((width, LANES), F32)],
        cost_estimate=cost(0.3),
        compiler_params=pltpu.CompilerParams(vmem_limit_bytes=32 << 20),
        name="turn_weights",
    )(after, w_qkv, w_proj, w_up, w_down, gain_attn, gain_mlp)


def cost(micros):
    return pl.CostEstimate(
        flops=int(micros * 1.1e9), bytes_accessed=int(micros * 3.3e6), transcendentals=0
    )


def dot_nn(left, right):
    return lax.dot_general(left, right, (((1,), (0,)), ((), ())), preferred_element_type=F32)


def dot_nt(left, right):
    return lax.dot_general(left, right, (((1,), (1,)), ((), ())), preferred_element_type=F32)


def eye(size):
    rows = lax.broadcasted_iota(jnp.int32, (size, size), 0)
    columns = lax.broadcasted_iota(jnp.int32, (size, size), 1)
    return (rows == columns).astype(BF16)


def gelu(value):
    return 0.5 * value * (1.0 + lax.erf(value * (0.5**0.5)))


HALF = SX * WY * WZ
QUARTER = HALF // 2
EARLY = 32


def moved(value, axis, steps):
    names = (axis,) if isinstance(axis, str) else tuple(axis)
    moves = (steps,) if isinstance(axis, str) else tuple(steps)
    counts = [lax.axis_size(name) for name in names]
    pairs = []
    for source in range(math.prod(counts)):
        left, target, stride = source, 0, 1
        for count, move in zip(reversed(counts), reversed(moves)):
            target += (left % count + move) % count * stride
            left //= count
            stride *= count
        pairs.append((source, target))
    return lax.ppermute(value, names, pairs)


def turned(value, steps):
    return pltpu.roll(value, steps % 8, axis=1)


def sublane(shape):
    return lax.broadcasted_iota(jnp.int32, shape, 1)


def pair_core(tall):
    number = tall.shape[0]
    split = tall.reshape(number // 2, 2, 8, LANES)
    first, second = split[:, 0], split[:, 1]
    return jnp.where(sublane(first.shape) < 4, turned(first, -2), turned(second, 2))


def quad_low(tall):
    number = tall.shape[0]
    split = tall.reshape(number // 4, 4, 8, LANES)
    at = sublane((number // 4, 8, LANES))
    low = jnp.where(at < 2, split[:, 0], turned(split[:, 1], 2))
    high = jnp.where(at < 6, turned(split[:, 2], 4), turned(split[:, 3], 6))
    return jnp.where(at < 4, low, high)


def pair_edge(tall, quads):
    number = tall.shape[0]
    split = tall.reshape(number // 4, 4, 8, LANES)
    at = sublane(quads.shape)
    even = jnp.where(
        at < 4,
        jnp.where(at < 2, turned(split[:, 0], 2), turned(quads, 2)),
        jnp.where(at < 6, turned(split[:, 1], -2), turned(quads, 4)),
    )
    odd = jnp.where(
        at < 4,
        jnp.where(at < 2, turned(split[:, 2], 2), turned(quads, -2)),
        jnp.where(at < 6, turned(split[:, 3], -2), quads),
    )
    return jnp.stack([even, odd], axis=1).reshape(number // 2, 8, LANES)


def unpair_edge(pairs):
    number = pairs.shape[0]
    split = pairs.reshape(number // 2, 2, 8, LANES)
    first, second = split[:, 0], split[:, 1]
    at = sublane(first.shape)
    near = jnp.where(
        at < 4,
        jnp.where(at < 2, first, turned(first, -2)),
        jnp.where(at < 6, turned(second, 4), turned(second, 2)),
    )
    far = jnp.where(
        at < 4,
        jnp.where(at < 2, turned(first, -2), turned(first, 4)),
        jnp.where(at < 6, turned(second, 2), second),
    )
    return near, far


def join_tall(low, core, near):
    number = low.shape[0]
    split = core.reshape(number, 2, 8, LANES)
    at = sublane(low.shape)
    parts = []
    for y in range(4):
        bottom = turned(low, -2 * y)
        top = turned(near, 6 - 2 * y)
        middle = turned(split[:, y // 2], 2 - 4 * (y % 2))
        parts.append(jnp.where(at < 2, bottom, jnp.where(at < 6, middle, top)))
    return jnp.stack(parts, axis=1).reshape(number * 4, 8, LANES)


def tall_of(ref, x_from, y_from, y_to, size_z=8):
    part = ref[x_from : x_from + SX, y_from * size_z : y_to * size_z, :]
    return part.astype(F32).reshape(-1, 8, LANES)


def rows_of(groups, *lead):
    return groups.reshape(*lead, -1, LANES).astype(BF16)


def as_groups(ref_value):
    return ref_value.astype(F32).reshape(-1, 8, LANES)


def low_kernel(tokens_ref, low_ref):
    size_y = low_ref.shape[1] // SZ
    for x_from in (0, SX):
        low = quad_low(tall_of(tokens_ref, x_from, 0, size_y))
        low_ref[x_from : x_from + SX] = rows_of(low, SX)


def shifted_kernel(
    tokens_ref, low_ref, region_ref, send_ref, own_ref, send_y_ref, own_y_ref
):
    windows = own_ref.shape[0]
    size_y = low_ref.shape[1] // SZ

    def core(x_from, start):
        return rows_of(pair_core(tall_of(tokens_ref, x_from, start, start + SY)))

    def edge(x_from, start):
        return rows_of(
            pair_edge(
                tall_of(tokens_ref, x_from, start, start + SY),
                tall_of(low_ref, x_from, start, start + SY, SZ),
            )
        )

    for at in range(windows):
        piece = (core, edge)[at % 2]
        for side in range(2):
            start = SY + at // 2 * WY + side * SY
            row = at * HALF + side * QUARTER
            send_ref[row : row + QUARTER] = piece(SX, start)
            own_ref[at, side * QUARTER : (side + 1) * QUARTER] = piece(0, start)
    for strip, start in enumerate((0, size_y - SY)):
        for half, x_from in enumerate((SX, 0)):
            for layer, piece in enumerate((core, edge)):
                row = ((strip * 2 + half) * 2 + layer) * QUARTER
                rows = piece(x_from, start)
                send_y_ref[row : row + QUARTER] = rows
                own_y_ref[row : row + QUARTER] = rows
    labels = region_ref[...].astype(F32).reshape(-1, size_y)
    blank = jnp.zeros((labels.shape[0], LANES - size_y), F32)
    labels = jnp.concatenate([labels, blank], axis=1).astype(BF16)
    send_ref[windows * HALF :] = labels
    send_y_ref[8 * QUARTER :] = labels


def across_pieces_kernel(own_ref, got_ref, send_ref):
    strip = 2 * QUARTER
    send_ref[:strip] = own_ref[2 * strip : 3 * strip]
    send_ref[strip : 2 * strip] = got_ref[:strip]
    send_ref[2 * strip : 3 * strip] = got_ref[2 * strip : 3 * strip]
    send_ref[3 * strip : 4 * strip] = own_ref[:strip]
    send_ref[4 * strip :] = got_ref[4 * strip :]


def windows_after(x16s, labels, spans, bias_refs, weights, ahead=4):
    gain_attn, w_qv_t, w_k, w_proj_t, w_up_t, w_down_t, gain_mlp = weights
    width = x16s[0].shape[1]
    size = width // HEADS
    scale = size**-0.5 * LOG2E
    eye_window = eye(WTOK)
    eye_width = eye(width)
    gain_mlp = jnp.concatenate([gain_mlp[...]] * (WTOK // LANES), axis=1)
    states = []
    for x16, (column, row), span in zip(x16s, labels, spans):
        x = x16.astype(F32)
        center = x - jnp.mean(x, axis=1, keepdims=True)
        spread = jnp.mean(center * center, axis=1, keepdims=True)
        normed = (center * lax.rsqrt(spread + 1e-05) * gain_attn[...]).astype(BF16)
        x_t = dot_nt(eye_width, x16[span])
        if span == slice(0, WTOK):
            qv_t = dot_nt(w_qv_t[...], normed).astype(BF16)
            q_t, v_t = qv_t[:width], qv_t[width:]
        else:
            q_t = dot_nt(w_qv_t[:width], normed[span]).astype(BF16)
            v_t = dot_nt(w_qv_t[width:], normed).astype(BF16)
        k = dot_nn(normed, w_k[...]).astype(BF16)
        lane = lax.broadcasted_iota(jnp.int32, column.shape, 1).astype(F32)
        k = jnp.concatenate([k, jnp.where(column == lane, 1.0, 0.0).astype(BF16)], axis=1)
        line = lax.broadcasted_iota(jnp.int32, (LANES, q_t.shape[1]), 0).astype(F32)
        fade = jnp.where(row[:, span] == line, 0.0, -1e10).astype(BF16)
        states.append((x_t, q_t, v_t, k, fade, span))
    tasks = [(at, head) for at in range(len(states)) for head in range(HEADS)]

    def scores(task):
        at, head = task
        _, q_t, _, k, fade, _ = states[at]
        pieces = [jnp.zeros((size, q_t.shape[1]), BF16)] * HEADS
        pieces[head] = q_t[head * size : (head + 1) * size]
        return dot_nn(k, jnp.concatenate(pieces + [fade], axis=0))

    def attend(task, raw):
        at, head = task
        _, _, v_t, _, _, span = states[at]
        bias = jnp.concatenate([ref[head, :, span] for ref in bias_refs], axis=0)
        score = raw * scale + bias
        weight = jnp.exp2(score - jnp.max(score, axis=0, keepdims=True))
        total = jnp.sum(weight, axis=0, keepdims=True)
        part = dot_nn(v_t[head * size : (head + 1) * size], weight.astype(BF16))
        return (part * (1.0 / total)).astype(BF16)

    raws, parts = {}, {}
    for at in range(min(ahead, len(tasks))):
        raws[at] = scores(tasks[at])
    for at, task in enumerate(tasks):
        if at + ahead < len(tasks):
            raws[at + ahead] = scores(tasks[at + ahead])
        parts[task] = attend(task, raws.pop(at))
    attended = [
        jnp.concatenate([parts[at, head] for head in range(HEADS)], axis=0)
        for at in range(len(states))
    ]
    residual = [state[0] for state in states]
    joined = WTOK // residual[0].shape[1]
    if joined > 1:
        group = lambda values: [
            jnp.concatenate(values[at : at + joined], axis=1) for at in range(0, len(values), joined)
        ]
        attended, residual = group(attended), group(residual)
    middles = [
        (x_t + dot_nn(w_proj_t[...], value)).astype(BF16).astype(F32)
        for x_t, value in zip(residual, attended)
    ]
    normeds = []
    for middle in middles:
        center = middle - jnp.mean(middle, axis=0, keepdims=True)
        spread = jnp.mean(center * center, axis=0, keepdims=True)
        normeds.append((center * lax.rsqrt(spread + 1e-05) * gain_mlp).astype(BF16))
    hiddens = [dot_nn(w_up_t[...], normed) for normed in normeds]
    hiddens = [gelu(hidden).astype(BF16) for hidden in hiddens]
    afters = [
        (middle + dot_nn(w_down_t[...], hidden)).astype(BF16)
        for middle, hidden in zip(middles, hiddens)
    ]
    return [dot_nt(eye_window, after).astype(BF16) for after in afters]


def window_labels(region, number):
    at = lax.broadcasted_iota(jnp.int32, (WTOK, region.shape[0]), 0)
    line = lax.broadcasted_iota(jnp.int32, (WTOK, region.shape[0]), 1)
    wanted = (at % HALF) // (SY * WZ) * 8 + (number % 2) * WZ + at % WZ
    lines = dot_nn((line == wanted).astype(BF16), region)
    at = lax.broadcasted_iota(jnp.int32, lines.shape, 0)
    y = lax.broadcasted_iota(jnp.int32, lines.shape, 1)
    wanted = number // 2 * WY + at // HALF * SY + at // WZ % SY
    lone = jnp.where(y == wanted, lines, 0.0).astype(BF16)
    ones = jnp.ones((LANES, lines.shape[1]), BF16)
    return dot_nt(lone, ones), dot_nt(ones[:8], lone)[:1]


def quarters(rows, start):
    at = start * QUARTER
    return rows[at : at + QUARTER]


def inside_kernel(near_ref, own_ref, early_ref, late_ref, *rest):
    weights, (back_ref, kept_ref) = rest[:7], rest[7:]
    windows = own_ref.shape[0]
    region = near_ref[windows * HALF :]
    x16s = []
    for at in range(windows):
        near, own = near_ref[at * HALF : (at + 1) * HALF], own_ref[at]
        x16s.append(
            jnp.concatenate([near[:QUARTER], own[:QUARTER], near[QUARTER:], own[QUARTER:]], axis=0)
        )
    labels = [window_labels(region, at) for at in range(windows)]
    afters = windows_after(x16s, labels, [slice(0, WTOK)] * windows, (early_ref, late_ref), weights)
    for at, after in enumerate(afters):
        for side in range(2):
            back_ref[at % 2, at // 2, side] = quarters(after, 2 * side)
            kept_ref[at % 2, at // 2, side] = quarters(after, 2 * side + 1)


def across_kernel(inside_ref, near_ref, own_ref, got_ref, early_ref, late_ref, *rest):
    weights, (back_ref, kept_ref) = rest[:7], rest[7:]
    size = near_ref.shape[0] - 8 * QUARTER
    windows = (inside_ref.shape[0] - size) // HALF
    x16s, labels, spans = [], [], []
    for place in range(2):
        region = (inside_ref[windows * HALF :], near_ref[8 * QUARTER :])[place]
        for layer in range(2):
            near = [quarters(near_ref, 4 * place + 2 * side + layer) for side in range(2)]
            if place == 0:
                own = [quarters(own_ref, 6 + layer), quarters(got_ref, 2 + layer)]
            else:
                own = [quarters(got_ref, 6 + layer), quarters(own_ref, 2 + layer)]
            x16s.append(jnp.concatenate([near[0], own[0], near[1], own[1]], axis=0))
            labels.append(window_labels(region, windows + layer))
            spans.append(slice(place * HALF, (place + 1) * HALF))
    afters = windows_after(x16s, labels, spans, (early_ref, late_ref), weights, ahead=8)
    for place, after in enumerate(afters):
        for layer in range(2):
            back_ref[layer, place] = quarters(after, 2 * layer)
            kept_ref[layer, place] = quarters(after, 2 * layer + 1)


def strips(size_y, inside_ref, across_ref):
    blocks = inside_ref.shape[1]
    for block in range(blocks):
        for side in range(2):
            yield SY + block * WY + side * SY, [inside_ref[layer, block, side] for layer in range(2)]
    yield size_y - SY, [across_ref[layer, 0] for layer in range(2)]
    yield 0, [across_ref[layer, 1] for layer in range(2)]


def far_kernel(inside_ref, across_ref, out_ref):
    size_y = out_ref.shape[1] // SZ
    for start, (_, edge) in strips(size_y, inside_ref, across_ref):
        far = unpair_edge(as_groups(edge))[1]
        out_ref[:, start * SZ : (start + SY) * SZ] = rows_of(far, SX)


def join_kernel(x_from, low_ref, inside_ref, across_ref, *rest):
    out_ref, block_ref, sent = rest[-3:]
    size_y = low_ref.shape[1] // SZ
    size_z = 8
    for start, (core, edge) in strips(size_y, inside_ref, across_ref):
        low = low_ref[:, start * SZ : (start + SY) * SZ, :].astype(F32).reshape(-1, 8, LANES)
        near = unpair_edge(as_groups(edge))[0]
        tall = join_tall(low, as_groups(core), near)
        block_ref[:, start * size_z : (start + SY) * size_z] = rows_of(tall, SX)
    move = pltpu.make_async_copy(block_ref, out_ref.at[x_from : x_from + SX], sent)
    move.start()
    move.wait()


def join_call(name, x_from, shape, *operands):
    given = len(operands) - 3
    return pl.pallas_call(
        functools.partial(join_kernel, x_from),
        in_specs=[pl.BlockSpec(memory_space=pltpu.VMEM)] * 3
        + [pl.BlockSpec(memory_space=pl.ANY)] * given,
        out_specs=pl.BlockSpec(memory_space=pl.ANY),
        out_shape=jax.ShapeDtypeStruct(shape, BF16),
        scratch_shapes=[pltpu.VMEM((SX,) + shape[1:], BF16), pltpu.SemaphoreType.DMA],
        input_output_aliases={3: 0} if given else {},
        cost_estimate=cost(0.7),
        compiler_params=pltpu.CompilerParams(vmem_limit_bytes=48 << 20),
        name=name,
    )(*operands)


def kernel_call(kernel, name, micros, outs, *operands):
    return pl.pallas_call(
        kernel,
        out_shape=[
            shape if hasattr(shape, "dtype") else jax.ShapeDtypeStruct(shape, BF16) for shape in outs
        ],
        cost_estimate=cost(micros),
        compiler_params=pltpu.CompilerParams(vmem_limit_bytes=48 << 20),
        name=name,
    )(*operands)


def per_device(
    tokens, region, rel_index, bias_table, gain_attn, w_qkv, w_proj, gain_mlp, w_up, w_down
):
    size_x, size_y, size_z, width = tokens.shape
    windows = 2 * (size_y // WY - 1)
    lines = size_x * size_z
    flat = tokens.reshape(size_x, size_y * size_z, width)
    low = kernel_call(low_kernel, "low_pieces", 0.2, [(size_x, size_y * SZ, width)], flat)[0]
    low = moved(low, "gz", -1)
    early, index, table, region, gain_attn, gain_mlp = first_bias(
        rel_index, bias_table.T, region.transpose(0, 2, 1), gain_attn[None], gain_mlp[None]
    )
    sent, own, strip, own_strip = kernel_call(
        shifted_kernel,
        "shifted_pieces",
        0.3,
        [
            (windows * HALF + lines, width),
            (windows, HALF, width),
            (8 * QUARTER + lines, width),
            (8 * QUARTER, width),
        ],
        flat,
        low,
        region,
    )
    near = moved(sent, "gx", 1)
    if lax.axis_size("gy") == 2:
        got = moved(strip, "gy", 1)
    else:
        got = jnp.concatenate(
            [moved(strip[: 4 * QUARTER], "gy", -1), moved(strip[4 * QUARTER :], "gy", 1)]
        )
    late = second_bias(index, table)
    fixed = (
        early, late, *turn_weights(late, w_qkv, w_proj, w_up, w_down, gain_attn, gain_mlp)
    )
    sent_across = kernel_call(
        across_pieces_kernel, "across_pieces", 0.2, [(8 * QUARTER + lines, width)], own_strip, got
    )[0]
    near_across = moved(sent_across, "gx", 1)
    halves = (2, windows // 2, 2, QUARTER, width)
    back, kept = kernel_call(
        inside_kernel, "inside_windows", 15, [halves, halves], near, own, *fixed
    )
    back = moved(back, "gx", -1)
    halves = (2, 2, QUARTER, width)
    back_across, kept_across = kernel_call(
        across_kernel, "across_windows", 2.3, [halves, halves], near, near_across, own_strip, got, *fixed
    )
    back_across = moved(back_across, "gx", -1)
    low_shape = [(SX, size_y * SZ, width)]
    low_own = kernel_call(far_kernel, "far_own", 0.1, low_shape, kept, kept_across)[0]
    out = join_call(
        "own_pieces", 0, flat.shape, moved(low_own, "gz", 1), kept, kept_across
    )
    low_back = kernel_call(far_kernel, "far_back", 0.1, low_shape, back, back_across)[0]
    out = join_call(
        "last_pieces", SX, flat.shape, moved(low_back, "gz", 1), back, back_across, out
    )
    return out.reshape(tokens.shape)


def solution(mesh):
    field = P(("cand", "gx"), "gy", "gz", None)
    placed = (field, P(("cand", "gx"), "gy", "gz")) + (P(),) * 8
    return jax.shard_map(
        per_device, mesh=mesh, in_specs=placed, out_specs=field, check_vma=False
    )
```

```python
import functools
import math

import jax
import jax.numpy as jnp
from jax import lax
from jax.experimental import pallas as pl
from jax.experimental.pallas import tpu as pltpu
from jax.sharding import PartitionSpec as P

HEADS = 4
WX = 8
WY = 8
WZ = 4
SX = 4
SY = 4
SZ = 2
WTOK = WX * WY * WZ
LANES = 128
F32 = jnp.float32
BF16 = jnp.bfloat16
LOG2E = 1.4426950408889634


def reordered(value):
    run = SY * WZ
    blocks = [
        value[(x * 2 + side) * run : (x * 2 + side + 1) * run] for side in range(2) for x in range(WX)
    ]
    return jnp.concatenate(blocks, axis=0)


def weights_kernel(
    _, w_qkv_ref, w_proj_ref, w_up_ref, w_down_ref, gain_attn_ref, gain_ref,
    gain_attn_out_ref, w_qv_t_ref, w_k_ref, w_proj_t_ref, w_up_t_ref, w_down_t_ref, gain_t_ref,
):
    width = w_proj_ref.shape[0]
    w_qv_t_ref[:width] = w_qkv_ref[:, :width].T
    w_qv_t_ref[width:] = w_qkv_ref[:, 2 * width :].T
    w_k_ref[...] = w_qkv_ref[:, width : 2 * width]
    w_proj_t_ref[...] = w_proj_ref[...].T
    w_up_t_ref[...] = w_up_ref[...].T
    w_down_t_ref[...] = w_down_ref[...].T
    gain_attn_out_ref[...] = gain_attn_ref[...]
    gain_t_ref[...] = jnp.broadcast_to(gain_ref[...], (LANES, width)).T


def gather_rows(index_ref, table_ref, bias_ref, start):
    chunks = table_ref.shape[1] // LANES
    for column in range(0, WTOK, LANES):
        for row in range(0, bias_ref.shape[1], 8):
            part = index_ref[start + row : start + row + 8, column : column + LANES]
            low = part & (LANES - 1)
            high = part >> 7
            found = [jnp.zeros((8, LANES), F32) for _ in range(HEADS)]
            for chunk in range(chunks):
                here = high == chunk
                for head in range(HEADS):
                    span = slice(chunk * LANES, (chunk + 1) * LANES)
                    line = jnp.broadcast_to(table_ref[head : head + 1, span], (8, LANES))
                    got = jnp.take_along_axis(line, low, axis=1, mode="promise_in_bounds")
                    found[head] = jnp.where(here, got, found[head])
            for head in range(HEADS):
                bias_ref[head, row : row + 8, column : column + LANES] = found[head] * LOG2E


def first_bias_kernel(
    given_index_ref, given_ref, region_ref, gain_ref, other_gain_ref,
    bias_ref, index_ref, table_ref, region_out_ref, gain_out_ref, other_gain_out_ref,
):
    region_out_ref[...] = region_ref[...]
    gain_out_ref[...] = gain_ref[...]
    other_gain_out_ref[...] = other_gain_ref[...]
    rows = given_ref.shape[1]
    table_ref[...] = jnp.zeros_like(table_ref)
    table_ref[:, :rows] = given_ref[...]
    index = reordered(reordered(given_index_ref[...].astype(F32)).T)
    index_ref[...] = index.astype(jnp.int32)
    gather_rows(index_ref, table_ref, bias_ref, 0)


def second_bias_kernel(index_ref, table_ref, bias_ref):
    gather_rows(index_ref, table_ref, bias_ref, WTOK - bias_ref.shape[1])


def first_bias(rel_index, table, region, gain_attn, gain_mlp):
    passed = (region, gain_attn, gain_mlp)
    padded = -(-table.shape[1] // LANES) * LANES
    return pl.pallas_call(
        first_bias_kernel,
        out_shape=[
            jax.ShapeDtypeStruct((HEADS, EARLY, WTOK), F32),
            jax.ShapeDtypeStruct((WTOK, WTOK), jnp.int32),
            jax.ShapeDtypeStruct((HEADS, padded), F32),
        ]
        + [jax.ShapeDtypeStruct(a.shape, a.dtype) for a in passed],
        cost_estimate=cost(0.7),
        compiler_params=pltpu.CompilerParams(vmem_limit_bytes=32 << 20),
        name="first_bias",
    )(rel_index, table, *passed)


def second_bias(index, table):
    return pl.pallas_call(
        second_bias_kernel,
        out_shape=jax.ShapeDtypeStruct((HEADS, WTOK - EARLY, WTOK), F32),
        cost_estimate=cost(1),
        compiler_params=pltpu.CompilerParams(vmem_limit_bytes=32 << 20),
        name="second_bias",
    )(index, table)


def turn_weights(after, w_qkv, w_proj, w_up, w_down, gain_attn, gain_mlp):
    width, hidden = w_up.shape
    shapes = [(2 * width, width), (width, width), (width, width), (hidden, width), (width, hidden)]
    return pl.pallas_call(
        weights_kernel,
        in_specs=[pl.BlockSpec(memory_space=pl.ANY)] + [pl.BlockSpec(memory_space=pltpu.VMEM)] * 6,
        out_shape=[jax.ShapeDtypeStruct((1, width), F32)]
        + [jax.ShapeDtypeStruct(shape, BF16) for shape in shapes]
        + [jax.ShapeDtypeStruct((width, LANES), F32)],
        cost_estimate=cost(0.3),
        compiler_params=pltpu.CompilerParams(vmem_limit_bytes=32 << 20),
        name="turn_weights",
    )(after, w_qkv, w_proj, w_up, w_down, gain_attn, gain_mlp)


def cost(micros):
    return pl.CostEstimate(
        flops=int(micros * 1.1e9), bytes_accessed=int(micros * 3.3e6), transcendentals=0
    )


def dot_nn(left, right):
    return lax.dot_general(left, right, (((1,), (0,)), ((), ())), preferred_element_type=F32)


def dot_nt(left, right):
    return lax.dot_general(left, right, (((1,), (1,)), ((), ())), preferred_element_type=F32)


def eye(size):
    rows = lax.broadcasted_iota(jnp.int32, (size, size), 0)
    columns = lax.broadcasted_iota(jnp.int32, (size, size), 1)
    return (rows == columns).astype(BF16)


def gelu(value):
    return 0.5 * value * (1.0 + lax.erf(value * (0.5**0.5)))


HALF = SX * WY * WZ
QUARTER = HALF // 2
EARLY = 16


def moved(value, axis, steps):
    names = (axis,) if isinstance(axis, str) else tuple(axis)
    moves = (steps,) if isinstance(axis, str) else tuple(steps)
    counts = [lax.axis_size(name) for name in names]
    pairs = []
    for source in range(math.prod(counts)):
        left, target, stride = source, 0, 1
        for count, move in zip(reversed(counts), reversed(moves)):
            target += (left % count + move) % count * stride
            left //= count
            stride *= count
        pairs.append((source, target))
    return lax.ppermute(value, names, pairs)


def turned(value, steps):
    return pltpu.roll(value, steps % 8, axis=1)


def sublane(shape):
    return lax.broadcasted_iota(jnp.int32, shape, 1)


def pair_core(tall):
    number = tall.shape[0]
    split = tall.reshape(number // 2, 2, 8, LANES)
    first, second = split[:, 0], split[:, 1]
    return jnp.where(sublane(first.shape) < 4, turned(first, -2), turned(second, 2))


def quad_low(tall):
    number = tall.shape[0]
    split = tall.reshape(number // 4, 4, 8, LANES)
    at = sublane((number // 4, 8, LANES))
    low = jnp.where(at < 2, split[:, 0], turned(split[:, 1], 2))
    high = jnp.where(at < 6, turned(split[:, 2], 4), turned(split[:, 3], 6))
    return jnp.where(at < 4, low, high)


def pair_edge(tall, quads):
    number = tall.shape[0]
    split = tall.reshape(number // 4, 4, 8, LANES)
    at = sublane(quads.shape)
    even = jnp.where(
        at < 4,
        jnp.where(at < 2, turned(split[:, 0], 2), turned(quads, 2)),
        jnp.where(at < 6, turned(split[:, 1], -2), turned(quads, 4)),
    )
    odd = jnp.where(
        at < 4,
        jnp.where(at < 2, turned(split[:, 2], 2), turned(quads, -2)),
        jnp.where(at < 6, turned(split[:, 3], -2), quads),
    )
    return jnp.stack([even, odd], axis=1).reshape(number // 2, 8, LANES)


def unpair_edge(pairs):
    number = pairs.shape[0]
    split = pairs.reshape(number // 2, 2, 8, LANES)
    first, second = split[:, 0], split[:, 1]
    at = sublane(first.shape)
    near = jnp.where(
        at < 4,
        jnp.where(at < 2, first, turned(first, -2)),
        jnp.where(at < 6, turned(second, 4), turned(second, 2)),
    )
    far = jnp.where(
        at < 4,
        jnp.where(at < 2, turned(first, -2), turned(first, 4)),
        jnp.where(at < 6, turned(second, 2), second),
    )
    return near, far


def join_tall(low, core, near):
    number = low.shape[0]
    split = core.reshape(number, 2, 8, LANES)
    at = sublane(low.shape)
    parts = []
    for y in range(4):
        bottom = turned(low, -2 * y)
        top = turned(near, 6 - 2 * y)
        middle = turned(split[:, y // 2], 2 - 4 * (y % 2))
        parts.append(jnp.where(at < 2, bottom, jnp.where(at < 6, middle, top)))
    return jnp.stack(parts, axis=1).reshape(number * 4, 8, LANES)


def tall_of(ref, x_from, y_from, y_to, size_z=8):
    part = ref[x_from : x_from + SX, y_from * size_z : y_to * size_z, :]
    return part.astype(F32).reshape(-1, 8, LANES)


def rows_of(groups, *lead):
    return groups.reshape(*lead, -1, LANES).astype(BF16)


def as_groups(ref_value):
    return ref_value.astype(F32).reshape(-1, 8, LANES)


def low_kernel(tokens_ref, low_ref):
    size_y = low_ref.shape[1] // SZ
    for x_from in (0, SX):
        low = quad_low(tall_of(tokens_ref, x_from, 0, size_y))
        low_ref[x_from : x_from + SX] = rows_of(low, SX)


def shifted_kernel(
    tokens_ref, low_ref, region_ref, send_ref, own_ref, send_y_ref, own_y_ref
):
    windows = own_ref.shape[0]
    size_y = low_ref.shape[1] // SZ

    def core(x_from, start):
        return rows_of(pair_core(tall_of(tokens_ref, x_from, start, start + SY)))

    def edge(x_from, start):
        return rows_of(
            pair_edge(
                tall_of(tokens_ref, x_from, start, start + SY),
                tall_of(low_ref, x_from, start, start + SY, SZ),
            )
        )

    for at in range(windows):
        piece = (core, edge)[at % 2]
        for side in range(2):
            start = SY + at // 2 * WY + side * SY
            row = at * HALF + side * QUARTER
            send_ref[row : row + QUARTER] = piece(SX, start)
            own_ref[at, side * QUARTER : (side + 1) * QUARTER] = piece(0, start)
    for strip, start in enumerate((0, size_y - SY)):
        for half, x_from in enumerate((SX, 0)):
            for layer, piece in enumerate((core, edge)):
                row = ((strip * 2 + half) * 2 + layer) * QUARTER
                rows = piece(x_from, start)
                send_y_ref[row : row + QUARTER] = rows
                own_y_ref[row : row + QUARTER] = rows
    labels = region_ref[...].astype(F32).reshape(-1, size_y)
    blank = jnp.zeros((labels.shape[0], LANES - size_y), F32)
    labels = jnp.concatenate([labels, blank], axis=1).astype(BF16)
    send_ref[windows * HALF :] = labels
    send_y_ref[8 * QUARTER :] = labels


def across_pieces_kernel(own_ref, got_ref, send_ref):
    strip = 2 * QUARTER
    send_ref[:strip] = own_ref[2 * strip : 3 * strip]
    send_ref[strip : 2 * strip] = got_ref[:strip]
    send_ref[2 * strip : 3 * strip] = got_ref[2 * strip : 3 * strip]
    send_ref[3 * strip : 4 * strip] = own_ref[:strip]
    send_ref[4 * strip :] = got_ref[4 * strip :]


def windows_after(x16s, labels, spans, bias_refs, weights, ahead=4):
    gain_attn, w_qv_t, w_k, w_proj_t, w_up_t, w_down_t, gain_mlp = weights
    width = x16s[0].shape[1]
    size = width // HEADS
    scale = size**-0.5 * LOG2E
    eye_window = eye(WTOK)
    eye_width = eye(width)
    gain_mlp = jnp.concatenate([gain_mlp[...]] * (WTOK // LANES), axis=1)
    states = []
    for x16, (column, row), span in zip(x16s, labels, spans):
        x = x16.astype(F32)
        center = x - jnp.mean(x, axis=1, keepdims=True)
        spread = jnp.mean(center * center, axis=1, keepdims=True)
        normed = (center * lax.rsqrt(spread + 1e-05) * gain_attn[...]).astype(BF16)
        x_t = dot_nt(eye_width, x16[span])
        if span == slice(0, WTOK):
            qv_t = dot_nt(w_qv_t[...], normed).astype(BF16)
            q_t, v_t = qv_t[:width], qv_t[width:]
        else:
            q_t = dot_nt(w_qv_t[:width], normed[span]).astype(BF16)
            v_t = dot_nt(w_qv_t[width:], normed).astype(BF16)
        k = dot_nn(normed, w_k[...]).astype(BF16)
        lane = lax.broadcasted_iota(jnp.int32, column.shape, 1).astype(F32)
        k = jnp.concatenate([k, jnp.where(column == lane, 1.0, 0.0).astype(BF16)], axis=1)
        line = lax.broadcasted_iota(jnp.int32, (LANES, q_t.shape[1]), 0).astype(F32)
        fade = jnp.where(row[:, span] == line, 0.0, -1e10).astype(BF16)
        states.append((x_t, q_t, v_t, k, fade, span))
    tasks = [(at, head) for at in range(len(states)) for head in range(HEADS)]

    def scores(task):
        at, head = task
        _, q_t, _, k, fade, _ = states[at]
        pieces = [jnp.zeros((size, q_t.shape[1]), BF16)] * HEADS
        pieces[head] = q_t[head * size : (head + 1) * size]
        return dot_nn(k, jnp.concatenate(pieces + [fade], axis=0))

    def attend(task, raw):
        at, head = task
        _, _, v_t, _, _, span = states[at]
        bias = jnp.concatenate([ref[head, :, span] for ref in bias_refs], axis=0)
        score = raw * scale + bias
        weight = jnp.exp2(score - jnp.max(score, axis=0, keepdims=True))
        total = jnp.sum(weight, axis=0, keepdims=True)
        part = dot_nn(v_t[head * size : (head + 1) * size], weight.astype(BF16))
        return (part * (1.0 / total)).astype(BF16)

    raws, parts = {}, {}
    for at in range(min(ahead, len(tasks))):
        raws[at] = scores(tasks[at])
    for at, task in enumerate(tasks):
        if at + ahead < len(tasks):
            raws[at + ahead] = scores(tasks[at + ahead])
        parts[task] = attend(task, raws.pop(at))
    attended = [
        jnp.concatenate([parts[at, head] for head in range(HEADS)], axis=0)
        for at in range(len(states))
    ]
    residual = [state[0] for state in states]
    joined = WTOK // residual[0].shape[1]
    if joined > 1:
        group = lambda values: [
            jnp.concatenate(values[at : at + joined], axis=1) for at in range(0, len(values), joined)
        ]
        attended, residual = group(attended), group(residual)
    middles = [
        (x_t + dot_nn(w_proj_t[...], value)).astype(BF16).astype(F32)
        for x_t, value in zip(residual, attended)
    ]
    normeds = []
    for middle in middles:
        center = middle - jnp.mean(middle, axis=0, keepdims=True)
        spread = jnp.mean(center * center, axis=0, keepdims=True)
        normeds.append((center * lax.rsqrt(spread + 1e-05) * gain_mlp).astype(BF16))
    hiddens = [dot_nn(w_up_t[...], normed) for normed in normeds]
    hiddens = [gelu(hidden).astype(BF16) for hidden in hiddens]
    afters = [
        (middle + dot_nn(w_down_t[...], hidden)).astype(BF16)
        for middle, hidden in zip(middles, hiddens)
    ]
    return [dot_nt(eye_window, after).astype(BF16) for after in afters]


def window_labels(region, number):
    at = lax.broadcasted_iota(jnp.int32, (WTOK, region.shape[0]), 0)
    line = lax.broadcasted_iota(jnp.int32, (WTOK, region.shape[0]), 1)
    wanted = (at % HALF) // (SY * WZ) * 8 + (number % 2) * WZ + at % WZ
    lines = dot_nn((line == wanted).astype(BF16), region)
    at = lax.broadcasted_iota(jnp.int32, lines.shape, 0)
    y = lax.broadcasted_iota(jnp.int32, lines.shape, 1)
    wanted = number // 2 * WY + at // HALF * SY + at // WZ % SY
    lone = jnp.where(y == wanted, lines, 0.0).astype(BF16)
    ones = jnp.ones((LANES, lines.shape[1]), BF16)
    return dot_nt(lone, ones), dot_nt(ones[:8], lone)[:1]


def quarters(rows, start):
    at = start * QUARTER
    return rows[at : at + QUARTER]


def inside_kernel(near_ref, own_ref, early_ref, late_ref, *rest):
    weights, (back_ref, kept_ref) = rest[:7], rest[7:]
    windows = own_ref.shape[0]
    region = near_ref[windows * HALF :]
    x16s = []
    for at in range(windows):
        near, own = near_ref[at * HALF : (at + 1) * HALF], own_ref[at]
        x16s.append(
            jnp.concatenate([near[:QUARTER], own[:QUARTER], near[QUARTER:], own[QUARTER:]], axis=0)
        )
    labels = [window_labels(region, at) for at in range(windows)]
    afters = windows_after(x16s, labels, [slice(0, WTOK)] * windows, (early_ref, late_ref), weights)
    for at, after in enumerate(afters):
        for side in range(2):
            back_ref[at % 2, at // 2, side] = quarters(after, 2 * side)
            kept_ref[at % 2, at // 2, side] = quarters(after, 2 * side + 1)


def across_kernel(inside_ref, near_ref, own_ref, got_ref, early_ref, late_ref, *rest):
    weights, (back_ref, kept_ref) = rest[:7], rest[7:]
    size = near_ref.shape[0] - 8 * QUARTER
    windows = (inside_ref.shape[0] - size) // HALF
    x16s, labels, spans = [], [], []
    for place in range(2):
        region = (inside_ref[windows * HALF :], near_ref[8 * QUARTER :])[place]
        for layer in range(2):
            near = [quarters(near_ref, 4 * place + 2 * side + layer) for side in range(2)]
            if place == 0:
                own = [quarters(own_ref, 6 + layer), quarters(got_ref, 2 + layer)]
            else:
                own = [quarters(got_ref, 6 + layer), quarters(own_ref, 2 + layer)]
            x16s.append(jnp.concatenate([near[0], own[0], near[1], own[1]], axis=0))
            labels.append(window_labels(region, windows + layer))
            spans.append(slice(place * HALF, (place + 1) * HALF))
    afters = windows_after(x16s, labels, spans, (early_ref, late_ref), weights, ahead=8)
    for place, after in enumerate(afters):
        for layer in range(2):
            back_ref[layer, place] = quarters(after, 2 * layer)
            kept_ref[layer, place] = quarters(after, 2 * layer + 1)


def strips(size_y, inside_ref, across_ref):
    blocks = inside_ref.shape[1]
    for block in range(blocks):
        for side in range(2):
            yield SY + block * WY + side * SY, [inside_ref[layer, block, side] for layer in range(2)]
    yield size_y - SY, [across_ref[layer, 0] for layer in range(2)]
    yield 0, [across_ref[layer, 1] for layer in range(2)]


def far_kernel(inside_ref, across_ref, out_ref):
    size_y = out_ref.shape[1] // SZ
    for start, (_, edge) in strips(size_y, inside_ref, across_ref):
        far = unpair_edge(as_groups(edge))[1]
        out_ref[:, start * SZ : (start + SY) * SZ] = rows_of(far, SX)


def join_kernel(x_from, low_ref, inside_ref, across_ref, *rest):
    out_ref, block_ref, sent = rest[-3:]
    size_y = low_ref.shape[1] // SZ
    size_z = 8
    for start, (core, edge) in strips(size_y, inside_ref, across_ref):
        low = low_ref[:, start * SZ : (start + SY) * SZ, :].astype(F32).reshape(-1, 8, LANES)
        near = unpair_edge(as_groups(edge))[0]
        tall = join_tall(low, as_groups(core), near)
        block_ref[:, start * size_z : (start + SY) * size_z] = rows_of(tall, SX)
    move = pltpu.make_async_copy(block_ref, out_ref.at[x_from : x_from + SX], sent)
    move.start()
    move.wait()


def join_call(name, x_from, shape, *operands):
    given = len(operands) - 3
    return pl.pallas_call(
        functools.partial(join_kernel, x_from),
        in_specs=[pl.BlockSpec(memory_space=pltpu.VMEM)] * 3
        + [pl.BlockSpec(memory_space=pl.ANY)] * given,
        out_specs=pl.BlockSpec(memory_space=pl.ANY),
        out_shape=jax.ShapeDtypeStruct(shape, BF16),
        scratch_shapes=[pltpu.VMEM((SX,) + shape[1:], BF16), pltpu.SemaphoreType.DMA],
        input_output_aliases={3: 0} if given else {},
        cost_estimate=cost(0.7),
        compiler_params=pltpu.CompilerParams(vmem_limit_bytes=48 << 20),
        name=name,
    )(*operands)


def kernel_call(kernel, name, micros, outs, *operands):
    return pl.pallas_call(
        kernel,
        out_shape=[
            shape if hasattr(shape, "dtype") else jax.ShapeDtypeStruct(shape, BF16) for shape in outs
        ],
        cost_estimate=cost(micros),
        compiler_params=pltpu.CompilerParams(vmem_limit_bytes=48 << 20),
        name=name,
    )(*operands)


def per_device(
    tokens, region, rel_index, bias_table, gain_attn, w_qkv, w_proj, gain_mlp, w_up, w_down
):
    size_x, size_y, size_z, width = tokens.shape
    windows = 2 * (size_y // WY - 1)
    lines = size_x * size_z
    flat = tokens.reshape(size_x, size_y * size_z, width)
    low = kernel_call(low_kernel, "low_pieces", 0.2, [(size_x, size_y * SZ, width)], flat)[0]
    low = moved(low, "gz", -1)
    early, index, table, region, gain_attn, gain_mlp = first_bias(
        rel_index, bias_table.T, region.transpose(0, 2, 1), gain_attn[None], gain_mlp[None]
    )
    sent, own, strip, own_strip = kernel_call(
        shifted_kernel,
        "shifted_pieces",
        0.3,
        [
            (windows * HALF + lines, width),
            (windows, HALF, width),
            (8 * QUARTER + lines, width),
            (8 * QUARTER, width),
        ],
        flat,
        low,
        region,
    )
    near = moved(sent, "gx", 1)
    if lax.axis_size("gy") == 2:
        got = moved(strip, "gy", 1)
    else:
        got = jnp.concatenate(
            [moved(strip[: 4 * QUARTER], "gy", -1), moved(strip[4 * QUARTER :], "gy", 1)]
        )
    late = second_bias(index, table)
    fixed = (
        early, late, *turn_weights(late, w_qkv, w_proj, w_up, w_down, gain_attn, gain_mlp)
    )
    sent_across = kernel_call(
        across_pieces_kernel, "across_pieces", 0.2, [(8 * QUARTER + lines, width)], own_strip, got
    )[0]
    near_across = moved(sent_across, "gx", 1)
    halves = (2, windows // 2, 2, QUARTER, width)
    back, kept = kernel_call(
        inside_kernel, "inside_windows", 15, [halves, halves], near, own, *fixed
    )
    back = moved(back, "gx", -1)
    halves = (2, 2, QUARTER, width)
    back_across, kept_across = kernel_call(
        across_kernel, "across_windows", 2.3, [halves, halves], near, near_across, own_strip, got, *fixed
    )
    back_across = moved(back_across, "gx", -1)
    low_shape = [(SX, size_y * SZ, width)]
    low_own = kernel_call(far_kernel, "far_own", 0.1, low_shape, kept, kept_across)[0]
    out = join_call(
        "own_pieces", 0, flat.shape, moved(low_own, "gz", 1), kept, kept_across
    )
    low_back = kernel_call(far_kernel, "far_back", 0.1, low_shape, back, back_across)[0]
    out = join_call(
        "last_pieces", SX, flat.shape, moved(low_back, "gz", 1), back, back_across, out
    )
    return out.reshape(tokens.shape)


def solution(mesh):
    field = P(("cand", "gx"), "gy", "gz", None)
    placed = (field, P(("cand", "gx"), "gy", "gz")) + (P(),) * 8
    return jax.shard_map(
        per_device, mesh=mesh, in_specs=placed, out_specs=field, check_vma=False
    )
```
